32 devices in a mesh: camp: 2 (over x), wide: 16 (over z, y, core).
Axes of the slice: x: 2, y: 2, z: 4, core: 2. Of those that a mesh axis runs over, the one named last changes fastest.
Arguments:
- coords: float32 [3, 16384], P(None, ('camp', 'wide')), parts along dimension 1, may hold values from 0 to 1
- intensity: float32 [16384], P(('camp', 'wide')), parts along dimension 0, may hold values from 0.3 to 3
- start: bfloat16 [16, 16384], P(None, ('camp', 'wide')), parts along dimension 1, may hold values from -6 to 6
Outputs:
- basis: float32 [16, 16384], P(None, ('camp', 'wide')), parts along dimension 1
- factor_out: float32 [32, 16], P('camp'), parts along dimension 0
The draws below stay inside these ranges and needn't reach their ends.
There are 2 independent parts, one for each index of `camp`. The reference program is written for one: setup_inputs(seed, part) draws one part's arguments, and reference() takes and returns one part's arrays. A program takes and returns all parts, laid end to end along the dimension named above; each array names one. Nothing has to cross between parts.
All inputs are finite; a program needn't handle non-finite values.
Results may differ from the reference program's by a relative error of at most 0.00075.
Values may be sent and summed in bfloat16 or wider, within the bound.
No kernel may reach another device: no remote copies, remote signals or barrier semaphores. Data moves between devices by JAX's collectives and lax.ppermute only.
A program may use at most 64 MiB of HBM per device.

```python
import math
import jax
import jax.numpy as jnp
from jax import lax

PTS_DEV = 512
COLS = 16
ITERS = 2
NPTS = 8192


def steps_of(rng, shape, shards, low, largest):
    factor_of, own = 1.0, jax.random.fold_in(rng, 6)
    for position, blocks in shards:
        heights = jnp.exp(jax.random.uniform(jax.random.fold_in(own, position), (blocks,), jnp.float32, low / len(shards), largest / len(shards)))
        factor_of = factor_of * jnp.repeat(heights, shape[position] // blocks).reshape([-1 if axis == position else 1 for axis in range(len(shape))])
    return factor_of


def bell_draw(rng, dims, spread, reach, cuts=(), kind=jnp.bfloat16):
    entries = jax.random.normal(rng, dims, jnp.float32) * spread
    if len(cuts) > 0:
        entries = steps_of(rng, dims, cuts, -0.22, 0.18) * entries
    return jnp.clip(entries, min=-reach, max=reach).astype(kind)


def setup_inputs(seed: int = 0, part: int = 0) -> dict:
    splits = jax.random.split(jax.random.key(seed), 4)
    part_keys = jax.random.split(jax.random.fold_in(splits[3], part), 4)
    return {
        "coords": jnp.clip(1.0 * jax.random.uniform(part_keys[0], (3, NPTS), jnp.float32) ** steps_of(part_keys[0], (3, NPTS), ((1, 16),), -0.2, 0.2), 0.0, 1.0),
        "intensity": jnp.clip(jnp.exp(math.log(3.0) - 2.3025851 * jax.random.uniform(part_keys[1], (NPTS,), jnp.float32) ** steps_of(part_keys[1], (NPTS,), ((0, 16),), -0.2, 0.2)), 0.3, 3.0),
        "start": bell_draw(part_keys[2], (COLS, NPTS), 1.0, 6.0, ((1, 16),)),
    }


rate_scale = 3.0 ** 0.5 / 0.15

def kernel_tile(left_xyz, left_scale, right_xyz, right_scale):
    squared = (left_xyz[0][:, None] - right_xyz[0][None, :]) ** 2
    squared = squared + (left_xyz[1][:, None] - right_xyz[1][None, :]) ** 2
    squared = squared + (left_xyz[2][:, None] - right_xyz[2][None, :]) ** 2
    scaled = rate_scale * jnp.sqrt(squared)
    value = left_scale[:, None] * right_scale[None, :] * (1.0 + scaled) * jnp.exp(-scaled)
    return value.astype(jnp.bfloat16)

def reference(coords, intensity, start):
    total_points = coords.shape[1]
    block_count = total_points // PTS_DEV
    basis = start
    factor_lower = jnp.zeros((COLS, COLS), jnp.float32)
    for sweep_index in range(ITERS):
        vectors = basis.astype(jnp.bfloat16)

        def row_block(block_index):
            anchor = (block_index * PTS_DEV).astype(jnp.int32)
            left_xyz = lax.dynamic_slice_in_dim(coords, anchor, PTS_DEV, 1)
            left_scale = lax.dynamic_slice_in_dim(intensity, anchor, PTS_DEV, 0)
            block_tile = kernel_tile(left_xyz, left_scale, coords, intensity)
            return jnp.dot(vectors.astype(jnp.float32), block_tile.T.astype(jnp.float32), preferred_element_type=jnp.float32)
        blocks = lax.map(row_block, jnp.arange(block_count, dtype=jnp.int32))
        product = blocks.transpose(1, 0, 2).reshape(COLS, total_points)
        gram = jnp.dot(product, product.T, precision=lax.Precision.HIGHEST) / total_points
        factor_lower = jnp.linalg.cholesky(gram)
        basis = lax.linalg.triangular_solve(factor_lower, product, left_side=True, lower=True)
    return (basis, factor_lower)
```

```python
import functools
import math

import jax
import jax.numpy as jnp
from jax import lax
from jax.experimental import pallas as pl
from jax.experimental.pallas import tpu as pltpu
from jax.sharding import PartitionSpec as P

LOG2E = 1.0 / math.log(2.0)
SCALE = 3.0**0.5 / 0.15 * LOG2E
LOG2_LN2 = math.log2(math.log(2.0))
TINY = 1e-20
FEATS = 8
STORE_LIMIT = 16 * 2**20
VMEM_LIMIT = 40 * 2**20


def split(value, parts):
    out = []
    for _ in range(parts):
        part = value.astype(jnp.bfloat16).astype(jnp.float32)
        out.append(part)
        value = value - part
    return out


def row_of(shape):
    return lax.broadcasted_iota(jnp.int32, shape, 0)


def norms(feats):
    whole = feats + jnp.roll(feats, -3, axis=0)
    squares = jnp.where(row_of(feats.shape) < 3, whole * whole, 0.0)
    return split(jnp.sum(squares, axis=0, keepdims=True), 3)


def stack_rows(rows, shape):
    index = row_of(shape)
    out = jnp.zeros(shape, jnp.float32)
    for k, row in rows.items():
        out = jnp.where(index == k, row, out)
    return out


def prepare_kernel(coords_ref, intensity_ref, start_ref, packed_ref, own_ref):
    points = coords_ref.shape[1]
    shape = (FEATS, points)
    centred = (coords_ref[...] - 0.5) * SCALE
    logs = jnp.log2(intensity_ref[...])
    hi, lo = split(centred, 2)
    log_hi, log_lo = split(logs, 2)
    feats = stack_rows(
        {
            **{k: hi[k : k + 1] for k in range(3)},
            **{3 + k: lo[k : k + 1] for k in range(3)},
            6: log_hi,
            7: log_lo,
        },
        shape,
    )
    packed_ref[...] = jnp.concatenate([start_ref[...].astype(jnp.float32), feats], axis=0).astype(jnp.bfloat16)
    n1, n2, n3 = norms(feats)
    p1, p2, p3 = split(logs + LOG2_LN2, 3)
    index = row_of(shape)
    double = -2.0 * feats
    with_hi = jnp.where(index < 3, double, jnp.where(index < 6, jnp.roll(double, 3, axis=0), 0.0))
    with_lo = jnp.where(index < 3, jnp.roll(double, -3, axis=0), jnp.where(index < 6, double, 0.0))
    with_norm = stack_rows({0: 1.0, 1: 1.0, 2: 1.0, 3: n1, 4: n2, 5: n3}, shape)
    with_log = stack_rows({6: 1.0, 7: 1.0}, shape)
    with_own = stack_rows({3: p1, 4: p2, 5: p3}, shape)
    distance = jnp.concatenate([with_hi, with_lo, with_norm], axis=0)
    weight = jnp.concatenate([with_log, jnp.zeros(shape, jnp.float32), with_own], axis=0)
    own_ref[...] = jnp.concatenate([distance, weight], axis=1).astype(jnp.bfloat16)


def prepare(coords, intensity, start):
    points = coords.shape[1]
    columns = start.shape[0]
    return pl.pallas_call(
        prepare_kernel,
        out_shape=(
            jax.ShapeDtypeStruct((columns + FEATS, points), jnp.bfloat16),
            jax.ShapeDtypeStruct((3 * FEATS, 2 * points), jnp.bfloat16),
        ),
        name="prepare",
    )(coords, intensity[None], start)


def block_product(packed, vectors, own_ref, cov_ref, first):
    points = packed.shape[1]
    columns = packed.shape[0] - FEATS
    feats = packed[columns:].astype(jnp.float32)
    n1, n2, n3 = norms(feats)
    with_norm = stack_rows({0: n1, 1: n2, 2: n3, 3: 1.0, 4: 1.0, 5: 1.0}, feats.shape)
    left = jnp.concatenate([feats, feats, with_norm], axis=0).astype(jnp.bfloat16)
    step = min(128, points)
    total = None
    for at in range(0, points, step):
        both = lax.dot_general(
            left[:, at : at + step], own_ref[...], (((0,), (0,)), ((), ())), preferred_element_type=jnp.float32
        )
        squared = jnp.maximum(both[:, :points], TINY)
        scaled = squared * lax.rsqrt(squared)
        value = (scaled + LOG2E) * jnp.exp2(both[:, points:] - scaled)
        tile = value.astype(jnp.bfloat16)
        if cov_ref is not None:
            cov_ref[pl.ds(first + at, step), :] = tile
        term = jnp.dot(vectors[:, at : at + step], tile, preferred_element_type=jnp.float32)
        total = term if total is None else total + term
    return total


def covariance_kernel(count, store, *refs):
    packed_refs, own_ref, sum_ref, out_ref = refs[:count], refs[count], refs[count + 1], refs[count + 2]
    cov_ref = refs[count + 3] if store else None
    points = own_ref.shape[1] // 2
    columns = sum_ref.shape[0]
    out_ref[...] = sum_ref[...]
    done = 0
    for ref in packed_refs:
        blocks = ref.shape[0]

        def step(k, carry, ref=ref, done=done):
            packed = ref[k]
            first = pl.multiple_of((done + k) * points, points)
            out_ref[...] += block_product(packed, packed[:columns], own_ref, cov_ref, first)
            return carry

        lax.fori_loop(0, blocks, step, 0)
        done += blocks


def covariance(packed, own, running, store):
    points = own.shape[1] // 2
    columns = running.shape[0]
    blocks = sum(p.shape[0] for p in packed)
    out_shape = [jax.ShapeDtypeStruct((columns, points), jnp.float32)]
    if store:
        out_shape.append(pltpu.VMEM((blocks * points, points), jnp.bfloat16))
    elements = blocks * points * points
    return pl.pallas_call(
        functools.partial(covariance_kernel, len(packed), store),
        out_shape=out_shape,
        compiler_params=pltpu.CompilerParams(vmem_limit_bytes=VMEM_LIMIT),
        cost_estimate=pl.CostEstimate(flops=8 * elements, bytes_accessed=2 * elements, transcendentals=2 * elements),
        name="covariance",
    )(*packed, own, running)


def gram_of(product):
    return lax.dot_general(
        product, product, (((1,), (1,)), ((), ())), precision=lax.Precision.HIGHEST, preferred_element_type=jnp.float32
    )


def second_kernel(count, *refs):
    vector_refs, cov_refs = refs[:count], refs[count : 2 * count]
    first_ref, out_ref, gram_ref = refs[2 * count :]
    points = out_ref.shape[1]
    columns = out_ref.shape[0]
    total = jnp.zeros(out_ref.shape, jnp.float32)
    for vectors, cov in zip(vector_refs, cov_refs):
        for k in range(vectors.shape[0]):
            total += jnp.dot(vectors[k], cov[pl.ds(k * points, points), :], preferred_element_type=jnp.float32)
    out_ref[...] = total
    gram_ref[:columns] = gram_of(total)
    gram_ref[columns:] = gram_of(first_ref[...])


def second(vectors, covs, first):
    columns, points = first.shape
    return pl.pallas_call(
        functools.partial(second_kernel, len(vectors)),
        out_shape=(
            jax.ShapeDtypeStruct((columns, points), jnp.float32),
            jax.ShapeDtypeStruct((2 * columns, columns), jnp.float32),
        ),
        compiler_params=pltpu.CompilerParams(vmem_limit_bytes=VMEM_LIMIT),
        name="second",
    )(*vectors, *covs, first)


def grams_kernel(second_ref, first_ref, gram_ref):
    columns = second_ref.shape[0]
    gram_ref[:columns] = gram_of(second_ref[...])
    gram_ref[columns:] = gram_of(first_ref[...])


def grams(second_product, first):
    columns = first.shape[0]
    return pl.pallas_call(
        grams_kernel, out_shape=jax.ShapeDtypeStruct((2 * columns, columns), jnp.float32), name="grams"
    )(second_product, first)


def eliminate(gram):
    size = gram.shape[0]
    wide = (size, 128)
    index = row_of(wide)
    cols = [jnp.broadcast_to(gram[:, k : k + 1], wide) for k in range(size)]
    multipliers, factor_cols = [], []
    scale = jnp.zeros(wide, jnp.float32)
    for k in range(size):
        pivot = jnp.broadcast_to(cols[k][k : k + 1], wide)
        root = 1.0 / jnp.sqrt(pivot)
        multiplier = jnp.where(index > k, cols[k] / pivot, 0.0)
        for j in range(k + 1, size):
            cols[j] = cols[j] - multiplier * jnp.broadcast_to(cols[j][k : k + 1], wide)
        multipliers.append(multiplier)
        factor_cols.append(jnp.where(index >= k, cols[k] * root, 0.0))
        scale = jnp.where(index == k, root, scale)
    return multipliers, factor_cols, scale


def finish_kernel(total_points, gram_ref, product_ref, basis_ref, factor_ref):
    size, points = product_ref.shape
    gram = gram_ref[...] / total_points
    steps, cols, scale = eliminate(gram[:size])
    first_steps, _, first_scale = eliminate(gram[size:])
    for at in range(0, points, 128):
        part = product_ref[:, at : at + 128]
        for k in range(size):
            part = part - steps[k] * part[k : k + 1]
        basis_ref[:, at : at + 128] = part * scale
    lane = lax.broadcasted_iota(jnp.int32, (size, 128), 1)
    factor = jnp.zeros((size, 128), jnp.float32)
    for k in range(size):
        factor = jnp.where(lane == k, cols[k], factor)
    for k in range(size):
        factor = factor - first_steps[k] * factor[k : k + 1]
    factor_ref[...] = (factor * first_scale)[:, :size]


def finish(gram, product, total_points):
    size, points = product.shape
    return pl.pallas_call(
        functools.partial(finish_kernel, total_points),
        out_shape=(
            jax.ShapeDtypeStruct((size, points), jnp.float32),
            jax.ShapeDtypeStruct((size, size), jnp.float32),
        ),
        name="finish",
    )(gram, product)


def rounds_of(width):
    bits = [1 << k for k in range(width.bit_length() - 1)][::-1]
    out = []
    while bits:
        take = 1 if len(bits) % 2 else 2
        group, bits = bits[:take], bits[take:]
        out.append([group[0]] if take == 1 else [group[1], group[0], group[0] + group[1]])
    return out


def exchange(value, distance, width):
    return lax.ppermute(value, "wide", [(k, k ^ distance) for k in range(width)])


def sum_all(value, width):
    for distances in rounds_of(width):
        got = [exchange(value, d, width) for d in distances]
        value = value + got[0]
        if len(got) > 1:
            value = value + (got[1] + got[2])
    return value


def gather_blocks(value, width):
    held = [value[None]]
    for distances in rounds_of(width):
        sent = held[0] if len(held) == 1 else jnp.concatenate(held, axis=0)
        held = held + [exchange(sent, d, width) for d in distances]
    return held


def body(coords, intensity, start):
    width = lax.axis_size("wide")
    columns, points = start.shape
    total_points = points * width
    packed, own = prepare(coords, intensity, start)
    zero = jnp.zeros((columns, points), jnp.float32)
    store = total_points * points * 2 <= STORE_LIMIT
    blocks = gather_blocks(packed, width)
    if store:
        running, groups, covs = zero, [], []
        rounds = len(rounds_of(width))
        at = 0
        for k in range(rounds + 1):
            size = 1 if k == 0 else len(rounds_of(width)[k - 1])
            running, cov = covariance(blocks[at : at + size], own, running, True)
            groups.append((at, size))
            covs.append(cov)
            at += size
        vectors = gather_blocks(running.astype(jnp.bfloat16), width)
        grouped = [
            vectors[a] if n == 1 else jnp.concatenate(vectors[a : a + n], axis=0) for a, n in groups
        ]
        product, gram = second(grouped, covs, running)
    else:
        everything = jnp.concatenate(blocks, axis=0)
        (running,) = covariance([everything], own, zero, False)
        vectors = jnp.concatenate(gather_blocks(running.astype(jnp.bfloat16), width), axis=0)
        again = jnp.concatenate([vectors, everything[:, columns:]], axis=1)
        (product,) = covariance([again], own, zero, False)
        gram = grams(product, running)
    return finish(sum_all(gram, width), product, float(total_points))


def solution(mesh):
    placed = (P(None, ("camp", "wide")), P(("camp", "wide")), P(None, ("camp", "wide")))
    return jax.shard_map(
        body,
        mesh=mesh,
        in_specs=placed,
        out_specs=(P(None, ("camp", "wide")), P("camp", None)),
        check_vma=False,
    )
```

```python
import functools
import math

import jax
import jax.numpy as jnp
from jax import lax
from jax.experimental import pallas as pl
from jax.experimental.pallas import tpu as pltpu
from jax.sharding import PartitionSpec as P

LOG2E = 1.0 / math.log(2.0)
SCALE = 3.0**0.5 / 0.15 * LOG2E
LOG2_LN2 = math.log2(math.log(2.0))
TINY = 1e-20
FEATS = 8
DEPTH = 4 * FEATS
LANES = 128
F32, BF16 = jnp.float32, jnp.bfloat16
NT = (((1,), (1,)), ((), ()))
PARAMS = pltpu.CompilerParams(vmem_limit_bytes=24 * 2**20)
SMALL = pltpu.CompilerParams(vmem_limit_bytes=8 * 2**20)


def split(value, parts):
    out = []
    for _ in range(parts):
        part = value.astype(BF16).astype(F32)
        out.append(part)
        value = value - part
    return out


def row_of(shape):
    return lax.broadcasted_iota(jnp.int32, shape, 0)


def stack_rows(rows, shape):
    index = row_of(shape)
    out = jnp.zeros(shape, F32)
    for k, row in rows.items():
        out = jnp.where(index == k, row, out)
    return out


def norms(feats):
    whole = feats + jnp.roll(feats, -3, axis=0)
    squares = jnp.where(row_of(feats.shape) < 3, whole * whole, 0.0)
    return split(jnp.sum(squares, axis=0, keepdims=True), 3)


def row_features(feats):
    shape = feats.shape
    n1, n2, n3 = norms(feats)
    p1, p2, p3 = split(feats[6:7] + feats[7:8] + LOG2_LN2, 3)
    index = row_of(shape)
    double = -2.0 * feats
    with_hi = jnp.where(index < 3, double, jnp.where(index < 6, jnp.roll(double, 3, axis=0), 0.0))
    with_lo = jnp.where(index < 3, jnp.roll(double, -3, axis=0), jnp.where(index < 6, double, 0.0))
    with_norm = stack_rows({0: 1.0, 1: 1.0, 2: 1.0, 3: n1, 4: n2, 5: n3}, shape)
    with_log = stack_rows({0: p1, 1: p2, 2: p3}, shape)
    rows = jnp.swapaxes(jnp.concatenate([with_hi, with_lo, with_norm, with_log], axis=0), 0, 1).astype(BF16)
    index = row_of((DEPTH, LANES))
    pick = jnp.where((index >= 3 * FEATS) & (index < 3 * FEATS + 3), 1.0, 0.0).astype(BF16)
    return rows, jnp.dot(rows, pick, preferred_element_type=F32)


def column_features(feats):
    n1, n2, n3 = norms(feats)
    with_norm = stack_rows({0: n1, 1: n2, 2: n3, 3: 1.0, 4: 1.0, 5: 1.0}, feats.shape)
    columns = jnp.concatenate([feats, feats, with_norm, jnp.zeros(feats.shape, F32)], axis=0).astype(BF16)
    return columns, feats[6:7] + feats[7:8]


def tile_of(rows, row_log, columns, column_log):
    points = columns.shape[1]
    squared = jnp.maximum(jnp.dot(rows, columns, preferred_element_type=F32), TINY)
    scaled = squared * lax.rsqrt(squared)
    logs = jnp.concatenate([row_log] * (points // LANES), axis=1) + column_log
    return ((scaled + LOG2E) * jnp.exp2(logs - scaled)).astype(BF16)


def prepare_kernel(coords_ref, intensity_ref, start_ref, packed_ref, feats_ref):
    hi, lo = split((coords_ref[...] - 0.5) * SCALE, 2)
    log_hi, log_lo = split(jnp.log2(intensity_ref[...]), 2)
    rows = {k: hi[k : k + 1] for k in range(3)}
    rows.update({3 + k: lo[k : k + 1] for k in range(3)})
    rows.update({6: log_hi, 7: log_lo})
    feats = stack_rows(rows, feats_ref.shape)
    packed_ref[...] = jnp.concatenate([start_ref[...].astype(F32), feats], axis=0).astype(BF16)
    feats_ref[...] = feats.astype(BF16)


def prepare(coords, intensity, start):
    columns, points = start.shape
    return pl.pallas_call(
        prepare_kernel,
        out_shape=(pltpu.VMEM((columns + FEATS, points), BF16), pltpu.VMEM((FEATS, points), BF16)),
        compiler_params=SMALL,
        name="prepare",
    )(coords, intensity[None], start)


def cost(elements):
    return pl.CostEstimate(flops=40 * elements, bytes_accessed=2 * elements, transcendentals=2 * elements)


def near_kernel(count, *refs):
    feats_refs, packed_ref = refs[:count], refs[count]
    rows_ref, logs_ref, cov_ref, part_ref = refs[count + 1 :]
    points = packed_ref.shape[1]
    size = packed_ref.shape[0] - FEATS
    packed = packed_ref[...]
    columns, column_log = column_features(packed[size:].astype(F32))
    made = [row_features(ref[...].astype(F32)) for ref in feats_refs]
    for k, (rows, row_log) in enumerate(made):
        at = slice(k * points, (k + 1) * points)
        rows_ref[at], logs_ref[at] = rows, row_log
        cov_ref[at] = tile_of(rows, row_log, columns, column_log)
        part_ref[k] = lax.dot_general(packed[:size], cov_ref[at], NT, preferred_element_type=F32)


def near(feats, packed):
    points = packed.shape[1]
    size = packed.shape[0] - FEATS
    total = len(feats) * points
    return pl.pallas_call(
        functools.partial(near_kernel, len(feats)),
        out_shape=(
            pltpu.VMEM((total, DEPTH), BF16),
            pltpu.VMEM((total, LANES), F32),
            pltpu.VMEM((total, points), BF16),
            pltpu.VMEM((len(feats), size, points), F32),
        ),
        compiler_params=PARAMS,
        cost_estimate=cost(total * points),
        name="near",
    )(*feats, packed)


def far_kernel(count, *refs):
    packed_refs = refs[:count]
    rows_ref, logs_ref, part_ref, cov_ref, sum_ref, sent_ref = refs[count:]
    points = packed_refs[0].shape[1]
    size = packed_refs[0].shape[0] - FEATS
    made = [column_features(ref[size:].astype(F32)) for ref in packed_refs]
    for k in range(part_ref.shape[0]):
        at = slice(k * points, (k + 1) * points)
        total = part_ref[k]
        for c, ref in enumerate(packed_refs):
            to = slice(c * points, (c + 1) * points)
            cov_ref[at, to] = tile_of(rows_ref[at], logs_ref[at], *made[c])
            total += lax.dot_general(ref[:size], cov_ref[at, to], NT, preferred_element_type=F32)
        sum_ref[k] = total
        sent_ref[k] = total.astype(BF16)


def far(packed, rows, logs, part):
    points = packed[0].shape[1]
    return pl.pallas_call(
        functools.partial(far_kernel, len(packed)),
        out_shape=(
            pltpu.VMEM((rows.shape[0], len(packed) * points), BF16),
            pltpu.VMEM(part.shape, F32),
            pltpu.VMEM(part.shape, BF16),
        ),
        compiler_params=PARAMS,
        cost_estimate=cost(rows.shape[0] * points * len(packed)),
        name="far",
    )(*packed, rows, logs, part)


def gram_of(product):
    return lax.dot_general(product, product, NT, precision=lax.Precision.HIGHEST, preferred_element_type=F32)


def second_kernel(own_ref, *refs):
    part_refs, near_ref, far_ref, outs, gram_ref = refs[:3], refs[3], refs[4], refs[5:-1], refs[-1]
    count, size, points = own_ref.shape
    totals = [jnp.zeros((2 * size, points), F32) for _ in outs]
    for k in range(count):
        a, b, c = (ref[k ^ (n + 1)].astype(F32) for n, ref in enumerate(part_refs))
        product = (own_ref[k] + a) + (b + c)
        if k == 0:
            gram_ref[...] = gram_of(product)
        vectors = jnp.concatenate(split(product, 2), axis=0).astype(BF16)
        at = slice(k * points, (k + 1) * points)
        for n in range(len(outs)):
            cov = near_ref[at] if n == 0 else far_ref[at, (n - 1) * points : n * points]
            totals[n] += jnp.dot(vectors, cov, preferred_element_type=F32)
    for ref, total in zip(outs, totals):
        ref[...] = total[:size] + total[size:]


def second(own, parts, near_cov, far_cov):
    _, size, points = own.shape
    blocks = 1 + far_cov.shape[1] // points
    return pl.pallas_call(
        second_kernel,
        out_shape=[pltpu.VMEM((size, points), F32)] * blocks + [pltpu.VMEM((size, size), F32)],
        compiler_params=PARAMS,
        name="second",
    )(own, *parts, near_cov, far_cov)


def gather_kernel(first_ref, own_ref, *refs):
    part_refs, (product_ref, gram_ref) = refs[:-2], refs[-2:]
    size = own_ref.shape[0]
    product = own_ref[...]
    for ref in part_refs:
        product += ref[...]
    product_ref[...] = product
    gram_ref[:size] = gram_of(product)
    gram_ref[size:] = first_ref[...]


def gather_parts(first_gram, own, parts):
    size, points = own.shape
    return pl.pallas_call(
        gather_kernel,
        out_shape=(pltpu.VMEM((size, points), F32), pltpu.VMEM((2 * size, size), F32)),
        compiler_params=SMALL,
        name="gather_parts",
    )(first_gram, own, *parts)


def row_kernel(packed_ref, feats_ref, out_ref):
    size = out_ref.shape[0]
    rows, row_log = row_features(feats_ref[...].astype(F32))
    out_ref[...] = jnp.zeros(out_ref.shape, F32)

    def step(k, carry):
        packed = packed_ref[k]
        columns, column_log = column_features(packed[size:].astype(F32))
        tile = tile_of(rows, row_log, columns, column_log)
        out_ref[...] += lax.dot_general(packed[:size], tile, NT, preferred_element_type=F32)
        return carry

    lax.fori_loop(0, packed_ref.shape[0], step, 0)


def row_product(packed, feats):
    _, rows, points = packed.shape
    return pl.pallas_call(
        row_kernel,
        out_shape=jax.ShapeDtypeStruct((rows - FEATS, points), F32),
        compiler_params=PARAMS,
        name="row_product",
    )(packed, feats)


def grams_kernel(second_ref, first_ref, gram_ref):
    size = second_ref.shape[0]
    gram_ref[:size] = gram_of(second_ref[...])
    gram_ref[size:] = gram_of(first_ref[...])


def grams(second_product, first_product):
    size = first_product.shape[0]
    return pl.pallas_call(
        grams_kernel,
        out_shape=jax.ShapeDtypeStruct((2 * size, size), F32),
        compiler_params=SMALL,
        name="grams",
    )(second_product, first_product)


def eliminate(gram):
    size = gram.shape[0]
    wide = (size, LANES)
    index = row_of(wide)
    cols = [jnp.broadcast_to(gram[:, k : k + 1], wide) for k in range(size)]
    multipliers, factor_cols = [], []
    scale = jnp.zeros(wide, F32)
    for k in range(size):
        pivot = jnp.broadcast_to(cols[k][k : k + 1], wide)
        root = 1.0 / jnp.sqrt(pivot)
        multiplier = jnp.where(index > k, cols[k] / pivot, 0.0)
        for j in range(k + 1, size):
            cols[j] = cols[j] - multiplier * jnp.broadcast_to(cols[j][k : k + 1], wide)
        multipliers.append(multiplier)
        factor_cols.append(jnp.where(index >= k, cols[k] * root, 0.0))
        scale = jnp.where(index == k, root, scale)
    return multipliers, factor_cols, scale


def finish_kernel(total_points, product_ref, *refs):
    gram_refs, (basis_ref, factor_ref) = refs[:-2], refs[-2:]
    size, points = product_ref.shape
    gram = gram_refs[0][...] + gram_refs[1][...]
    if len(gram_refs) > 2:
        gram = gram + (gram_refs[2][...] + gram_refs[3][...])
    gram = gram / total_points
    steps, cols, scale = eliminate(gram[:size])
    first_steps, _, first_scale = eliminate(gram[size:])
    for at in range(0, points, LANES):
        part = product_ref[:, at : at + LANES]
        for k in range(size):
            part = part - steps[k] * part[k : k + 1]
        basis_ref[:, at : at + LANES] = part * scale
    lane = lax.broadcasted_iota(jnp.int32, (size, LANES), 1)
    factor = jnp.zeros((size, LANES), F32)
    for k in range(size):
        factor = jnp.where(lane == k, cols[k], factor)
    for k in range(size):
        factor = factor - first_steps[k] * factor[k : k + 1]
    factor_ref[...] = (factor * first_scale)[:, :size]


def finish(product, gram_parts, total_points):
    size, points = product.shape
    return pl.pallas_call(
        functools.partial(finish_kernel, total_points),
        out_shape=(jax.ShapeDtypeStruct((size, points), F32), jax.ShapeDtypeStruct((size, size), F32)),
        compiler_params=SMALL,
        name="finish",
    )(product, *gram_parts)


def rounds_of(width):
    bits = [1 << k for k in range(width.bit_length() - 1)][::-1]
    out = []
    while bits:
        take = 1 if len(bits) % 2 else 2
        group, bits = bits[:take], bits[take:]
        out.append([group[0]] if take == 1 else [group[1], group[0], group[0] + group[1]])
    return out


def exchange(value, distance, width):
    return lax.ppermute(value, "wide", [(k, k ^ distance) for k in range(width)])


def sum_parts(value, width):
    rounds = rounds_of(width)
    for n, distances in enumerate(rounds):
        parts = [value] + [exchange(value, d, width) for d in distances]
        if n == len(rounds) - 1:
            return parts
        value = parts[0] + parts[1]
        if len(parts) > 2:
            value = value + (parts[2] + parts[3])


def gather_blocks(value, width):
    held = value[None]
    for distances in rounds_of(width):
        held = jnp.concatenate([held] + [exchange(held, d, width) for d in distances], axis=0)
    return held


def body(coords, intensity, start):
    width = lax.axis_size("wide")
    size, points = start.shape
    packed, feats = prepare(coords, intensity, start)
    rounds = rounds_of(width)
    if [len(r) for r in rounds] == [3, 3]:
        far_steps, near_steps = rounds
        near_feats = [feats] + [exchange(feats, d, width) for d in near_steps]
        far_packed = [exchange(packed, d, width) for d in far_steps]
        rows, logs, near_cov, part = near(near_feats, packed)
        far_cov, own, sent = far(far_packed, rows, logs, part)
        parts = [exchange(own if d == 1 else sent, d, width) for d in near_steps]
        *products, first_gram = second(own, parts, near_cov, far_cov)
        got = [exchange(p, d, width) for p, d in zip(products[1:], far_steps)]
        product, gram = gather_parts(first_gram, products[0], got)
    else:
        everything = gather_blocks(packed, width)
        first_product = row_product(everything, feats)
        vectors = gather_blocks(first_product.astype(BF16), width)
        product = row_product(jnp.concatenate([vectors, everything[:, size:]], axis=1), feats)
        gram = grams(product, first_product)
    return finish(product, sum_parts(gram, width), float(points * width))


def solution(mesh):
    placed = (P(None, ("camp", "wide")), P(("camp", "wide")), P(None, ("camp", "wide")))
    return jax.shard_map(
        body,
        mesh=mesh,
        in_specs=placed,
        out_specs=(P(None, ("camp", "wide")), P("camp", None)),
        check_vma=False,
    )
```

```python
import functools
import math

import jax
import jax.numpy as jnp
from jax import lax
from jax.experimental import pallas as pl
from jax.experimental.pallas import tpu as pltpu
from jax.sharding import PartitionSpec as P

LOG2E = 1.0 / math.log(2.0)
SCALE = 3.0**0.5 / 0.15 * LOG2E
LOG2_LN2 = math.log2(math.log(2.0))
SMALLEST = 1e-4
FEATS = 8
DEPTH = 4 * FEATS
LANES = 128
F32, BF16 = jnp.float32, jnp.bfloat16
NT = (((1,), (1,)), ((), ()))
PARAMS = pltpu.CompilerParams(vmem_limit_bytes=24 * 2**20)
SMALL = pltpu.CompilerParams(vmem_limit_bytes=8 * 2**20)


def split(value, parts):
    out = []
    for _ in range(parts):
        part = value.astype(BF16).astype(F32)
        out.append(part)
        value = value - part
    return out


def row_of(shape):
    return lax.broadcasted_iota(jnp.int32, shape, 0)


def stack_rows(rows, shape):
    index = row_of(shape)
    out = jnp.zeros(shape, F32)
    for k, row in rows.items():
        out = jnp.where(index == k, row, out)
    return out


def norms(feats):
    whole = feats + jnp.roll(feats, -3, axis=0)
    squares = jnp.where(row_of(feats.shape) < 3, whole * whole, 0.0)
    return split(jnp.sum(squares, axis=0, keepdims=True), 3)


def row_features(feats):
    shape = feats.shape
    n1, n2, n3 = norms(feats)
    p1, p2, p3 = split(feats[6:7] + feats[7:8] + LOG2_LN2, 3)
    index = row_of(shape)
    double = -2.0 * feats
    with_hi = jnp.where(index < 3, double, jnp.where(index < 6, jnp.roll(double, 3, axis=0), 0.0))
    with_lo = jnp.where(index < 3, jnp.roll(double, -3, axis=0), jnp.where(index < 6, double, 0.0))
    with_norm = stack_rows({0: 1.0, 1: 1.0, 2: 1.0, 3: n1, 4: n2, 5: n3}, shape)
    with_log = stack_rows({0: p1, 1: p2, 2: p3}, shape)
    rows = jnp.swapaxes(jnp.concatenate([with_hi, with_lo, with_norm, with_log], axis=0), 0, 1).astype(BF16)
    index = row_of((DEPTH, LANES))
    pick = jnp.where((index >= 3 * FEATS) & (index < 3 * FEATS + 3), 1.0, 0.0).astype(BF16)
    return rows, jnp.dot(rows, pick, preferred_element_type=F32)


def column_features(feats):
    n1, n2, n3 = norms(feats)
    with_norm = stack_rows({0: n1, 1: n2, 2: n3, 3: 1.0, 4: 1.0, 5: 1.0}, feats.shape)
    columns = jnp.concatenate([feats, feats, with_norm, jnp.zeros(feats.shape, F32)], axis=0).astype(BF16)
    return columns, feats[6:7] + feats[7:8]


def tile_of(rows, row_log, columns, column_log):
    points = columns.shape[1]
    squared = jnp.dot(rows, columns, preferred_element_type=F32)
    scaled = squared * lax.rsqrt(jnp.maximum(squared, SMALLEST))
    logs = jnp.concatenate([row_log] * (points // LANES), axis=1) + column_log
    return ((scaled + LOG2E) * jnp.exp2(logs - scaled)).astype(BF16)


def prepare_kernel(*refs):
    sources, (packed_ref, feats_ref), buffers, sems = refs[:3], refs[3:5], refs[5:8], refs[8]
    copies = [pltpu.make_async_copy(a, b, sems.at[n]) for n, (a, b) in enumerate(zip(sources, buffers))]
    for copy in copies:
        copy.start()
    for copy in copies:
        copy.wait()
    coords_ref, intensity_ref, start_ref = buffers
    hi, lo = split((coords_ref[...] - 0.5) * SCALE, 2)
    log_hi, log_lo = split(jnp.log2(intensity_ref[...]), 2)
    rows = {k: hi[k : k + 1] for k in range(3)}
    rows.update({3 + k: lo[k : k + 1] for k in range(3)})
    rows.update({6: log_hi, 7: log_lo})
    feats = stack_rows(rows, feats_ref.shape)
    packed_ref[...] = jnp.concatenate([start_ref[...].astype(F32), feats], axis=0).astype(BF16)
    feats_ref[...] = feats.astype(BF16)


def prepare(coords, intensity, start):
    columns, points = start.shape
    return pl.pallas_call(
        prepare_kernel,
        in_specs=[pl.BlockSpec(memory_space=pltpu.HBM)] * 3,
        out_shape=(pltpu.VMEM((columns + FEATS, points), BF16), pltpu.VMEM((FEATS, points), BF16)),
        scratch_shapes=[
            pltpu.VMEM(coords.shape, F32),
            pltpu.VMEM((1, points), F32),
            pltpu.VMEM(start.shape, BF16),
            pltpu.SemaphoreType.DMA((3,)),
        ],
        name="prepare",
    )(coords, intensity[None], start)


def cost(elements):
    return pl.CostEstimate(flops=40 * elements, bytes_accessed=2 * elements, transcendentals=2 * elements)


def near_kernel(count, feats_ref, *refs):
    packed_refs, (columns_ref, logs_ref, cov_ref, part_ref) = refs[:count], refs[count:]
    size, points = part_ref.shape
    rows, row_log = row_features(feats_ref[...].astype(F32))
    made = [column_features(ref[...].astype(F32)[size:]) for ref in packed_refs]
    total = jnp.zeros(part_ref.shape, F32)
    for c, ref in enumerate(packed_refs):
        to = slice(c * points, (c + 1) * points)
        columns_ref[:, to], logs_ref[:, to] = made[c]
        cov_ref[:, to] = tile_of(rows, row_log, *made[c])
        total += lax.dot_general(ref[:size], cov_ref[:, to], NT, preferred_element_type=F32)
    part_ref[...] = total


def near(feats, packed):
    rows, points = packed[0].shape
    total = len(packed) * points
    return pl.pallas_call(
        functools.partial(near_kernel, len(packed)),
        out_shape=(
            pltpu.VMEM((DEPTH, total), BF16),
            pltpu.VMEM((1, total), F32),
            pltpu.VMEM((points, total), BF16),
            pltpu.VMEM((rows - FEATS, points), F32),
        ),
        compiler_params=PARAMS,
        cost_estimate=cost(total * points),
        name="near",
    )(feats, *packed)


def far_kernel(count, near_ref, columns_ref, logs_ref, *refs):
    feats_refs, packed_refs, (cov_ref, sum_ref, sent_ref) = refs[:count], refs[count:-3], refs[-3:]
    size, points = near_ref.shape
    made = [row_features(ref[...].astype(F32)) for ref in feats_refs]
    sum_ref[0] = near_ref[...]
    sent_ref[0] = near_ref[...].astype(BF16)
    for k in range(count):
        at = slice(k * points, (k + 1) * points)
        total = jnp.zeros(near_ref.shape, F32)
        for c, ref in enumerate(packed_refs):
            to = slice(c * points, (c + 1) * points)
            cov_ref[at, to] = tile_of(*made[k], columns_ref[:, to], logs_ref[:, to])
            total += lax.dot_general(ref[:size], cov_ref[at, to], NT, preferred_element_type=F32)
        sum_ref[k + 1] = total
        sent_ref[k + 1] = total.astype(BF16)


def far(near_part, columns, logs, feats, packed):
    size, points = near_part.shape
    rows = len(feats) * points
    return pl.pallas_call(
        functools.partial(far_kernel, len(feats)),
        out_shape=(
            pltpu.VMEM((rows, columns.shape[1]), BF16),
            pltpu.VMEM((1 + len(feats), size, points), F32),
            pltpu.VMEM((1 + len(feats), size, points), BF16),
        ),
        compiler_params=PARAMS,
        cost_estimate=cost(rows * columns.shape[1]),
        name="far",
    )(near_part, columns, logs, *feats, *packed)


def gram_of(product):
    return lax.dot_general(product, product, NT, precision=lax.Precision.HIGHEST, preferred_element_type=F32)


def second_kernel(own_ref, *refs):
    part_refs, near_ref, far_ref, outs, gram_ref = refs[:3], refs[3], refs[4], refs[5:-1], refs[-1]
    count, size, points = own_ref.shape
    totals = [jnp.zeros((2 * size, points), F32) for _ in outs]
    for k in range(count):
        a, b, c = (ref[k ^ (n + 1)].astype(F32) for n, ref in enumerate(part_refs))
        product = (own_ref[k] + a) + (b + c)
        if k == 0:
            gram_ref[...] = gram_of(product)
        vectors = jnp.concatenate(split(product, 2), axis=0).astype(BF16)
        for n in range(len(outs)):
            to = slice(n * points, (n + 1) * points)
            cov = near_ref[:, to] if k == 0 else far_ref[(k - 1) * points : k * points, to]
            totals[n] += jnp.dot(vectors, cov, preferred_element_type=F32)
    for ref, total in zip(outs, totals):
        ref[...] = total[:size] + total[size:]


def second(own, parts, near_cov, far_cov):
    _, size, points = own.shape
    blocks = far_cov.shape[1] // points
    return pl.pallas_call(
        second_kernel,
        out_shape=[pltpu.VMEM((size, points), F32)] * blocks + [pltpu.VMEM((size, size), F32)],
        compiler_params=PARAMS,
        name="second",
    )(own, *parts, near_cov, far_cov)


def gather_kernel(first_ref, own_ref, *refs):
    part_refs, (product_ref, gram_ref) = refs[:-2], refs[-2:]
    size = own_ref.shape[0]
    product = own_ref[...]
    for ref in part_refs:
        product += ref[...]
    product_ref[...] = product
    gram_ref[:size] = gram_of(product)
    gram_ref[size:] = first_ref[...]


def gather_parts(first_gram, own, parts):
    size, points = own.shape
    return pl.pallas_call(
        gather_kernel,
        out_shape=(pltpu.VMEM((size, points), F32), pltpu.VMEM((2 * size, size), F32)),
        compiler_params=SMALL,
        name="gather_parts",
    )(first_gram, own, *parts)


def row_kernel(packed_ref, feats_ref, out_ref):
    size = out_ref.shape[0]
    rows, row_log = row_features(feats_ref[...].astype(F32))
    out_ref[...] = jnp.zeros(out_ref.shape, F32)

    def step(k, carry):
        packed = packed_ref[k]
        columns, column_log = column_features(packed[size:].astype(F32))
        tile = tile_of(rows, row_log, columns, column_log)
        out_ref[...] += lax.dot_general(packed[:size], tile, NT, preferred_element_type=F32)
        return carry

    lax.fori_loop(0, packed_ref.shape[0], step, 0)


def row_product(packed, feats):
    _, rows, points = packed.shape
    return pl.pallas_call(
        row_kernel,
        out_shape=jax.ShapeDtypeStruct((rows - FEATS, points), F32),
        compiler_params=PARAMS,
        name="row_product",
    )(packed, feats)


def grams_kernel(second_ref, first_ref, gram_ref):
    size = second_ref.shape[0]
    gram_ref[:size] = gram_of(second_ref[...])
    gram_ref[size:] = gram_of(first_ref[...])


def grams(second_product, first_product):
    size = first_product.shape[0]
    return pl.pallas_call(
        grams_kernel,
        out_shape=jax.ShapeDtypeStruct((2 * size, size), F32),
        compiler_params=SMALL,
        name="grams",
    )(second_product, first_product)


def eliminate(gram):
    size = gram.shape[0]
    wide = (size, LANES)
    index = row_of(wide)
    cols = [jnp.broadcast_to(gram[:, k : k + 1], wide) for k in range(size)]
    multipliers, factor_cols = [], []
    scale = jnp.zeros(wide, F32)
    for k in range(size):
        pivot = jnp.broadcast_to(cols[k][k : k + 1], wide)
        root = 1.0 / jnp.sqrt(pivot)
        multiplier = jnp.where(index > k, cols[k] / pivot, 0.0)
        for j in range(k + 1, size):
            cols[j] = cols[j] - multiplier * jnp.broadcast_to(cols[j][k : k + 1], wide)
        multipliers.append(multiplier)
        factor_cols.append(jnp.where(index >= k, cols[k] * root, 0.0))
        scale = jnp.where(index == k, root, scale)
    return multipliers, factor_cols, scale


def finish_kernel(total_points, product_ref, *refs):
    gram_refs, (basis_ref, factor_ref) = refs[:-2], refs[-2:]
    size, points = product_ref.shape
    gram = gram_refs[0][...] + gram_refs[1][...]
    if len(gram_refs) > 2:
        gram = gram + (gram_refs[2][...] + gram_refs[3][...])
    gram = gram / total_points
    steps, cols, scale = eliminate(gram[:size])
    first_steps, _, first_scale = eliminate(gram[size:])
    for at in range(0, points, LANES):
        part = product_ref[:, at : at + LANES]
        for k in range(size):
            part = part - steps[k] * part[k : k + 1]
        basis_ref[:, at : at + LANES] = part * scale
    lane = lax.broadcasted_iota(jnp.int32, (size, LANES), 1)
    factor = jnp.zeros((size, LANES), F32)
    for k in range(size):
        factor = jnp.where(lane == k, cols[k], factor)
    for k in range(size):
        factor = factor - first_steps[k] * factor[k : k + 1]
    factor_ref[...] = (factor * first_scale)[:, :size]


def finish(product, gram_parts, total_points):
    size, points = product.shape
    return pl.pallas_call(
        functools.partial(finish_kernel, total_points),
        out_shape=(jax.ShapeDtypeStruct((size, points), F32), jax.ShapeDtypeStruct((size, size), F32)),
        compiler_params=SMALL,
        name="finish",
    )(product, *gram_parts)


def rounds_of(width):
    bits = [1 << k for k in range(width.bit_length() - 1)][::-1]
    out = []
    while bits:
        take = 1 if len(bits) % 2 else 2
        group, bits = bits[:take], bits[take:]
        out.append([group[0]] if take == 1 else [group[1], group[0], group[0] + group[1]])
    return out


def exchange(value, distance, width):
    return lax.ppermute(value, "wide", [(k, k ^ distance) for k in range(width)])


def sum_parts(value, width):
    rounds = rounds_of(width)[::-1]
    rounds = rounds[:1] + [[d + 1 if d.bit_count() == 1 else d ^ 1 for d in r] for r in rounds[1:]]
    for n, distances in enumerate(rounds):
        parts = [value] + [exchange(value, d, width) for d in distances]
        if n == len(rounds) - 1:
            return parts
        value = parts[1] + parts[0]
        if len(parts) > 2:
            value = value + (parts[3] + parts[2])


def gather_blocks(value, width):
    held = value[None]
    for distances in rounds_of(width):
        held = jnp.concatenate([held] + [exchange(held, d, width) for d in distances], axis=0)
    return held


def body(coords, intensity, start):
    width = lax.axis_size("wide")
    size, points = start.shape
    packed, feats = prepare(coords, intensity, start)
    if width == 16:
        near_steps, far_steps = (1, 2, 3), (8, 13, 5)
        blocks = [packed] + [exchange(packed, d, width) for d in far_steps]
        others = [exchange(feats, d, width) for d in near_steps]
        features, logs, near_cov, part = near(feats, blocks)
        far_cov, own, sent = far(part, features, logs, others, blocks)
        parts = [exchange(own if d == 1 else sent, d, width) for d in near_steps]
        *products, first_gram = second(own, parts, near_cov, far_cov)
        got = [exchange(p, d, width) for p, d in zip(products[1:], far_steps)]
        product, gram = gather_parts(first_gram, products[0], got)
    else:
        everything = gather_blocks(packed, width)
        first_product = row_product(everything, feats)
        vectors = gather_blocks(first_product.astype(BF16), width)
        product = row_product(jnp.concatenate([vectors, everything[:, size:]], axis=1), feats)
        gram = grams(product, first_product)
    return finish(product, sum_parts(gram, width), float(points * width))


def solution(mesh):
    placed = (P(None, ("camp", "wide")), P(("camp", "wide")), P(None, ("camp", "wide")))
    return jax.shard_map(
        body,
        mesh=mesh,
        in_specs=placed,
        out_specs=(P(None, ("camp", "wide")), P("camp", None)),
        check_vma=False,
    )
```

```python
import functools
import math

import jax
import jax.numpy as jnp
from jax import lax
from jax.experimental import pallas as pl
from jax.experimental.pallas import tpu as pltpu
from jax.sharding import PartitionSpec as P

LOG2E = 1.0 / math.log(2.0)
SCALE = 3.0**0.5 / 0.15 * LOG2E
LOG2_LN2 = math.log2(math.log(2.0))
SMALLEST = 1e-4
FEATS = 8
DEPTH = 4 * FEATS
LANES = 128
F32, BF16 = jnp.float32, jnp.bfloat16
NT = (((1,), (1,)), ((), ()))
PARAMS = pltpu.CompilerParams(vmem_limit_bytes=24 * 2**20)
SMALL = pltpu.CompilerParams(vmem_limit_bytes=8 * 2**20)


def split(value, parts):
    out = []
    for _ in range(parts):
        part = value.astype(BF16).astype(F32)
        out.append(part)
        value = value - part
    return out


def row_of(shape):
    return lax.broadcasted_iota(jnp.int32, shape, 0)


def stack_rows(rows, shape):
    index = row_of(shape)
    out = jnp.zeros(shape, F32)
    for k, row in rows.items():
        out = jnp.where(index == k, row, out)
    return out


def norms(feats):
    whole = feats + jnp.roll(feats, -3, axis=0)
    squares = jnp.where(row_of(feats.shape) < 3, whole * whole, 0.0)
    return split(jnp.sum(squares, axis=0, keepdims=True), 3)


def row_features(feats):
    shape = feats.shape
    n1, n2, n3 = norms(feats)
    p1, p2, p3 = split(feats[6:7] + feats[7:8] + LOG2_LN2, 3)
    index = row_of(shape)
    double = -2.0 * feats
    with_hi = jnp.where(index < 3, double, jnp.where(index < 6, jnp.roll(double, 3, axis=0), 0.0))
    with_lo = jnp.where(index < 3, jnp.roll(double, -3, axis=0), jnp.where(index < 6, double, 0.0))
    with_norm = stack_rows({0: 1.0, 1: 1.0, 2: 1.0, 3: n1, 4: n2, 5: n3}, shape)
    with_log = stack_rows({0: p1, 1: p2, 2: p3}, shape)
    rows = jnp.swapaxes(jnp.concatenate([with_hi, with_lo, with_norm, with_log], axis=0), 0, 1).astype(BF16)
    index = row_of((DEPTH, LANES))
    pick = jnp.where((index >= 3 * FEATS) & (index < 3 * FEATS + 3), 1.0, 0.0).astype(BF16)
    return rows, jnp.dot(rows, pick, preferred_element_type=F32)


def column_features(feats):
    n1, n2, n3 = norms(feats)
    with_norm = stack_rows({0: n1, 1: n2, 2: n3, 3: 1.0, 4: 1.0, 5: 1.0}, feats.shape)
    columns = jnp.concatenate([feats, feats, with_norm, jnp.zeros(feats.shape, F32)], axis=0).astype(BF16)
    return columns, feats[6:7] + feats[7:8]


def tile_of(rows, row_log, columns, column_log):
    points = columns.shape[1]
    squared = jnp.dot(rows, columns, preferred_element_type=F32)
    scaled = squared * lax.rsqrt(jnp.maximum(squared, SMALLEST))
    logs = jnp.concatenate([row_log] * (points // LANES), axis=1) + column_log
    return ((scaled + LOG2E) * jnp.exp2(logs - scaled)).astype(BF16)


def prepare_kernel(*refs):
    sources, (packed_ref, feats_ref), buffers, sems = refs[:3], refs[3:5], refs[5:8], refs[8]
    copies = [pltpu.make_async_copy(a, b, sems.at[n]) for n, (a, b) in enumerate(zip(sources, buffers))]
    for copy in copies:
        copy.start()
    for copy in copies:
        copy.wait()
    coords_ref, intensity_ref, start_ref = buffers
    hi, lo = split((coords_ref[...] - 0.5) * SCALE, 2)
    log_hi, log_lo = split(jnp.log2(intensity_ref[...]), 2)
    rows = {k: hi[k : k + 1] for k in range(3)}
    rows.update({3 + k: lo[k : k + 1] for k in range(3)})
    rows.update({6: log_hi, 7: log_lo})
    feats = stack_rows(rows, feats_ref.shape)
    packed_ref[...] = jnp.concatenate([start_ref[...].astype(F32), feats], axis=0).astype(BF16)
    feats_ref[...] = feats.astype(BF16)


def prepare(coords, intensity, start):
    columns, points = start.shape
    return pl.pallas_call(
        prepare_kernel,
        in_specs=[pl.BlockSpec(memory_space=pltpu.HBM)] * 3,
        out_shape=(pltpu.VMEM((columns + FEATS, points), BF16), pltpu.VMEM((FEATS, points), BF16)),
        scratch_shapes=[
            pltpu.VMEM(coords.shape, F32),
            pltpu.VMEM((1, points), F32),
            pltpu.VMEM(start.shape, BF16),
            pltpu.SemaphoreType.DMA((3,)),
        ],
        name="prepare",
    )(coords, intensity[None], start)


def cost(elements):
    return pl.CostEstimate(flops=40 * elements, bytes_accessed=2 * elements, transcendentals=2 * elements)


def near_kernel(count, feats_ref, *refs):
    packed_refs, (rows_ref, row_logs_ref, columns_ref, logs_ref, cov_ref, part_ref) = refs[:count], refs[count:]
    size, points = part_ref.shape
    rows, row_log = row_features(feats_ref[...].astype(F32))
    rows_ref[...], row_logs_ref[...] = rows, row_log
    made = [column_features(ref[...].astype(F32)[size:]) for ref in packed_refs]
    total = jnp.zeros(part_ref.shape, F32)
    for c, ref in enumerate(packed_refs):
        to = slice(c * points, (c + 1) * points)
        columns_ref[:, to], logs_ref[:, to] = made[c]
        cov_ref[:, to] = tile_of(rows, row_log, *made[c])
        total += lax.dot_general(ref[:size], cov_ref[:, to], NT, preferred_element_type=F32)
    part_ref[...] = total


def near(feats, packed):
    rows, points = packed[0].shape
    total = len(packed) * points
    return pl.pallas_call(
        functools.partial(near_kernel, len(packed)),
        out_shape=(
            pltpu.VMEM((points, DEPTH), BF16),
            pltpu.VMEM((points, LANES), F32),
            pltpu.VMEM((DEPTH, total), BF16),
            pltpu.VMEM((1, total), F32),
            pltpu.VMEM((points, total), BF16),
            pltpu.VMEM((rows - FEATS, points), F32),
        ),
        compiler_params=PARAMS,
        cost_estimate=cost(total * points),
        name="near",
    )(feats, *packed)


def far_kernel(count, near_ref, rows_ref, row_logs_ref, columns_ref, logs_ref, last_ref, *refs):
    feats_refs, packed_refs, (edge_ref, cov_ref, sum_ref, sent_ref) = refs[:count], refs[count:-4], refs[-4:]
    size, points = near_ref.shape
    made = [row_features(ref[...].astype(F32)) for ref in feats_refs]
    columns, logs = [], []
    for c in range(len(packed_refs)):
        to = slice(c * points, (c + 1) * points)
        columns.append(columns_ref[:, to])
        logs.append(logs_ref[:, to])
    last, last_log = column_features(last_ref[...].astype(F32)[size:])
    columns.append(last)
    logs.append(last_log)
    sources = list(packed_refs) + [last_ref]
    edge_ref[...] = tile_of(rows_ref[...], row_logs_ref[...], last, last_log)
    total = near_ref[...] + lax.dot_general(last_ref[:size], edge_ref[...], NT, preferred_element_type=F32)
    sum_ref[0] = total
    sent_ref[0] = total.astype(BF16)
    for k in range(count):
        at = slice(k * points, (k + 1) * points)
        total = jnp.zeros(near_ref.shape, F32)
        for c, ref in enumerate(sources):
            to = slice(c * points, (c + 1) * points)
            cov_ref[at, to] = tile_of(*made[k], columns[c], logs[c])
            total += lax.dot_general(ref[:size], cov_ref[at, to], NT, preferred_element_type=F32)
        sum_ref[k + 1] = total
        sent_ref[k + 1] = total.astype(BF16)


def far(near_part, rows, row_logs, columns, logs, feats, packed, last):
    size, points = near_part.shape
    height, wide = len(feats) * points, (len(packed) + 1) * points
    return pl.pallas_call(
        functools.partial(far_kernel, len(feats)),
        out_shape=(
            pltpu.VMEM((points, points), BF16),
            pltpu.VMEM((height, wide), BF16),
            pltpu.VMEM((1 + len(feats), size, points), F32),
            pltpu.VMEM((1 + len(feats), size, points), BF16),
        ),
        compiler_params=PARAMS,
        cost_estimate=cost((height + points) * wide),
        name="far",
    )(near_part, rows, row_logs, columns, logs, last, *feats, *packed)


def gram_of(product):
    return lax.dot_general(product, product, NT, precision=lax.Precision.HIGHEST, preferred_element_type=F32)


def second_kernel(own_ref, *refs):
    part_refs, near_ref, edge_ref, far_ref, outs, gram_ref = refs[:3], refs[3], refs[4], refs[5], refs[6:-1], refs[-1]
    count, size, points = own_ref.shape
    totals = [jnp.zeros((2 * size, points), F32) for _ in outs]
    for k in range(count):
        a, b, c = (ref[k ^ (n + 1)].astype(F32) for n, ref in enumerate(part_refs))
        product = (own_ref[k] + a) + (b + c)
        if k == 0:
            gram_ref[...] = gram_of(product)
        vectors = jnp.concatenate(split(product, 2), axis=0).astype(BF16)
        for n in range(len(outs)):
            to = slice(n * points, (n + 1) * points)
            if k == 0:
                cov = near_ref[:, to] if n < len(outs) - 1 else edge_ref[...]
            else:
                cov = far_ref[(k - 1) * points : k * points, to]
            totals[n] += jnp.dot(vectors, cov, preferred_element_type=F32)
    for ref, total in zip(outs, totals):
        ref[...] = total[:size] + total[size:]


def second(own, parts, near_cov, edge_cov, far_cov):
    _, size, points = own.shape
    blocks = far_cov.shape[1] // points
    return pl.pallas_call(
        second_kernel,
        out_shape=[pltpu.VMEM((size, points), F32)] * blocks + [pltpu.VMEM((size, size), F32)],
        compiler_params=PARAMS,
        name="second",
    )(own, *parts, near_cov, edge_cov, far_cov)


def gather_kernel(first_ref, own_ref, *refs):
    part_refs, (product_ref, gram_ref) = refs[:-2], refs[-2:]
    size = own_ref.shape[0]
    product = own_ref[...]
    for ref in part_refs:
        product += ref[...]
    product_ref[...] = product
    gram_ref[:size] = gram_of(product)
    gram_ref[size:] = first_ref[...]


def gather_parts(first_gram, own, parts):
    size, points = own.shape
    return pl.pallas_call(
        gather_kernel,
        out_shape=(pltpu.VMEM((size, points), F32), pltpu.VMEM((2 * size, size), F32)),
        compiler_params=SMALL,
        name="gather_parts",
    )(first_gram, own, *parts)


def row_kernel(packed_ref, feats_ref, out_ref):
    size = out_ref.shape[0]
    rows, row_log = row_features(feats_ref[...].astype(F32))
    out_ref[...] = jnp.zeros(out_ref.shape, F32)

    def step(k, carry):
        packed = packed_ref[k]
        columns, column_log = column_features(packed[size:].astype(F32))
        tile = tile_of(rows, row_log, columns, column_log)
        out_ref[...] += lax.dot_general(packed[:size], tile, NT, preferred_element_type=F32)
        return carry

    lax.fori_loop(0, packed_ref.shape[0], step, 0)


def row_product(packed, feats):
    _, rows, points = packed.shape
    return pl.pallas_call(
        row_kernel,
        out_shape=jax.ShapeDtypeStruct((rows - FEATS, points), F32),
        compiler_params=PARAMS,
        name="row_product",
    )(packed, feats)


def grams_kernel(second_ref, first_ref, gram_ref):
    size = second_ref.shape[0]
    gram_ref[:size] = gram_of(second_ref[...])
    gram_ref[size:] = gram_of(first_ref[...])


def grams(second_product, first_product):
    size = first_product.shape[0]
    return pl.pallas_call(
        grams_kernel,
        out_shape=jax.ShapeDtypeStruct((2 * size, size), F32),
        compiler_params=SMALL,
        name="grams",
    )(second_product, first_product)


def eliminate(gram):
    size = gram.shape[0]
    wide = (size, LANES)
    index = row_of(wide)
    cols = [jnp.broadcast_to(gram[:, k : k + 1], wide) for k in range(size)]
    multipliers, factor_cols = [], []
    scale = jnp.zeros(wide, F32)
    for k in range(size):
        pivot = jnp.broadcast_to(cols[k][k : k + 1], wide)
        root = 1.0 / jnp.sqrt(pivot)
        multiplier = jnp.where(index > k, cols[k] / pivot, 0.0)
        for j in range(k + 1, size):
            cols[j] = cols[j] - multiplier * jnp.broadcast_to(cols[j][k : k + 1], wide)
        multipliers.append(multiplier)
        factor_cols.append(jnp.where(index >= k, cols[k] * root, 0.0))
        scale = jnp.where(index == k, root, scale)
    return multipliers, factor_cols, scale


def finish_kernel(total_points, product_ref, *refs):
    gram_refs, (basis_ref, factor_ref) = refs[:-2], refs[-2:]
    size, points = product_ref.shape
    gram = gram_refs[0][...] + gram_refs[1][...]
    if len(gram_refs) > 2:
        gram = gram + (gram_refs[2][...] + gram_refs[3][...])
    gram = gram / total_points
    steps, cols, scale = eliminate(gram[:size])
    first_steps, _, first_scale = eliminate(gram[size:])
    for at in range(0, points, LANES):
        part = product_ref[:, at : at + LANES]
        for k in range(size):
            part = part - steps[k] * part[k : k + 1]
        basis_ref[:, at : at + LANES] = part * scale
    lane = lax.broadcasted_iota(jnp.int32, (size, LANES), 1)
    factor = jnp.zeros((size, LANES), F32)
    for k in range(size):
        factor = jnp.where(lane == k, cols[k], factor)
    for k in range(size):
        factor = factor - first_steps[k] * factor[k : k + 1]
    factor_ref[...] = (factor * first_scale)[:, :size]


def finish(product, gram_parts, total_points):
    size, points = product.shape
    return pl.pallas_call(
        functools.partial(finish_kernel, total_points),
        out_shape=(jax.ShapeDtypeStruct((size, points), F32), jax.ShapeDtypeStruct((size, size), F32)),
        compiler_params=SMALL,
        name="finish",
    )(product, *gram_parts)


def rounds_of(width):
    bits = [1 << k for k in range(width.bit_length() - 1)][::-1]
    out = []
    while bits:
        take = 1 if len(bits) % 2 else 2
        group, bits = bits[:take], bits[take:]
        out.append([group[0]] if take == 1 else [group[1], group[0], group[0] + group[1]])
    return out


def exchange(value, distance, width):
    return lax.ppermute(value, "wide", [(k, k ^ distance) for k in range(width)])


def sum_parts(value, width):
    rounds = rounds_of(width)[::-1]
    rounds = rounds[:1] + [[d + 1 if d.bit_count() == 1 else d ^ 1 for d in r] for r in rounds[1:]]
    for n, distances in enumerate(rounds):
        parts = [value] + [exchange(value, d, width) for d in distances]
        if n == len(rounds) - 1:
            return parts
        value = parts[1] + parts[0]
        if len(parts) > 2:
            value = value + (parts[3] + parts[2])


def gather_blocks(value, width):
    held = value[None]
    for distances in rounds_of(width):
        held = jnp.concatenate([held] + [exchange(held, d, width) for d in distances], axis=0)
    return held


def body(coords, intensity, start):
    width = lax.axis_size("wide")
    size, points = start.shape
    packed, feats = prepare(coords, intensity, start)
    if width == 16:
        near_steps, far_steps = (1, 2, 3), (8, 13, 5)
        blocks = [packed] + [exchange(packed, d, width) for d in far_steps]
        others = [exchange(feats, d, width) for d in near_steps]
        *features, near_cov, part = near(feats, blocks[:-1])
        edge_cov, far_cov, own, sent = far(part, *features, others, blocks[:-1], blocks[-1])
        parts = [exchange(own if d == 1 else sent, d, width) for d in near_steps]
        *products, first_gram = second(own, parts, near_cov, edge_cov, far_cov)
        got = [exchange(p, d, width) for p, d in zip(products[1:], far_steps)]
        product, gram = gather_parts(first_gram, products[0], got)
    else:
        everything = gather_blocks(packed, width)
        first_product = row_product(everything, feats)
        vectors = gather_blocks(first_product.astype(BF16), width)
        product = row_product(jnp.concatenate([vectors, everything[:, size:]], axis=1), feats)
        gram = grams(product, first_product)
    return finish(product, sum_parts(gram, width), float(points * width))


def solution(mesh):
    placed = (P(None, ("camp", "wide")), P(("camp", "wide")), P(None, ("camp", "wide")))
    return jax.shard_map(
        body,
        mesh=mesh,
        in_specs=placed,
        out_specs=(P(None, ("camp", "wide")), P("camp", None)),
        check_vma=False,
    )
```

```python
import functools
import math

import jax
import jax.numpy as jnp
from jax import lax
from jax.experimental import pallas as pl
from jax.experimental.pallas import tpu as pltpu
from jax.sharding import PartitionSpec as P

LOG2E = 1.0 / math.log(2.0)
SCALE = 3.0**0.5 / 0.15 * LOG2E
LOG2_LN2 = math.log2(math.log(2.0))
SMALLEST = 1e-4
FEATS = 8
DEPTH = 4 * FEATS
LANES = 128
F32, BF16 = jnp.float32, jnp.bfloat16
NT = (((1,), (1,)), ((), ()))
PARAMS = pltpu.CompilerParams(vmem_limit_bytes=24 * 2**20)
SMALL = pltpu.CompilerParams(vmem_limit_bytes=8 * 2**20)


def split(value, parts):
    out = []
    for _ in range(parts):
        part = value.astype(BF16).astype(F32)
        out.append(part)
        value = value - part
    return out


def row_of(shape):
    return lax.broadcasted_iota(jnp.int32, shape, 0)


def stack_rows(rows, shape):
    index = row_of(shape)
    out = jnp.zeros(shape, F32)
    for k, row in rows.items():
        out = jnp.where(index == k, row, out)
    return out


def norms(feats):
    whole = feats + jnp.roll(feats, -3, axis=0)
    squares = jnp.where(row_of(feats.shape) < 3, whole * whole, 0.0)
    return split(jnp.sum(squares, axis=0, keepdims=True), 3)


def row_features(feats):
    shape = feats.shape
    n1, n2, n3 = norms(feats)
    p1, p2, p3 = split(feats[6:7] + feats[7:8] + LOG2_LN2, 3)
    index = row_of(shape)
    double = -2.0 * feats
    with_hi = jnp.where(index < 3, double, jnp.where(index < 6, jnp.roll(double, 3, axis=0), 0.0))
    with_lo = jnp.where(index < 3, jnp.roll(double, -3, axis=0), jnp.where(index < 6, double, 0.0))
    with_norm = stack_rows({0: 1.0, 1: 1.0, 2: 1.0, 3: n1, 4: n2, 5: n3}, shape)
    with_log = stack_rows({0: p1, 1: p2, 2: p3}, shape)
    rows = jnp.swapaxes(jnp.concatenate([with_hi, with_lo, with_norm, with_log], axis=0), 0, 1).astype(BF16)
    index = row_of((DEPTH, LANES))
    pick = jnp.where((index >= 3 * FEATS) & (index < 3 * FEATS + 3), 1.0, 0.0).astype(BF16)
    return rows, jnp.dot(rows, pick, preferred_element_type=F32)


def column_features(feats):
    n1, n2, n3 = norms(feats)
    with_norm = stack_rows({0: n1, 1: n2, 2: n3, 3: 1.0, 4: 1.0, 5: 1.0}, feats.shape)
    columns = jnp.concatenate([feats, feats, with_norm, jnp.zeros(feats.shape, F32)], axis=0).astype(BF16)
    return columns, feats[6:7] + feats[7:8]


def tile_of(rows, row_log, columns, column_log):
    points = columns.shape[1]
    squared = jnp.dot(rows, columns, preferred_element_type=F32)
    scaled = squared * lax.rsqrt(jnp.maximum(squared, SMALLEST))
    logs = jnp.concatenate([row_log] * (points // LANES), axis=1) + column_log
    return ((scaled + LOG2E) * jnp.exp2(logs - scaled)).astype(BF16)


def prepare_kernel(*refs):
    sources, (packed_ref, feats_ref), buffers, sems = refs[:3], refs[3:5], refs[5:8], refs[8]
    copies = [pltpu.make_async_copy(a, b, sems.at[n]) for n, (a, b) in enumerate(zip(sources, buffers))]
    for copy in copies:
        copy.start()
    for copy in copies:
        copy.wait()
    coords_ref, intensity_ref, start_ref = buffers
    hi, lo = split((coords_ref[...] - 0.5) * SCALE, 2)
    log_hi, log_lo = split(jnp.log2(intensity_ref[...]), 2)
    rows = {k: hi[k : k + 1] for k in range(3)}
    rows.update({3 + k: lo[k : k + 1] for k in range(3)})
    rows.update({6: log_hi, 7: log_lo})
    feats = stack_rows(rows, feats_ref.shape)
    packed_ref[...] = jnp.concatenate([start_ref[...].astype(F32), feats], axis=0).astype(BF16)
    feats_ref[...] = feats.astype(BF16)


def prepare(coords, intensity, start):
    columns, points = start.shape
    return pl.pallas_call(
        prepare_kernel,
        in_specs=[pl.BlockSpec(memory_space=pltpu.HBM)] * 3,
        out_shape=(pltpu.VMEM((columns + FEATS, points), BF16), pltpu.VMEM((FEATS, points), BF16)),
        scratch_shapes=[
            pltpu.VMEM(coords.shape, F32),
            pltpu.VMEM((1, points), F32),
            pltpu.VMEM(start.shape, BF16),
            pltpu.SemaphoreType.DMA((3,)),
        ],
        name="prepare",
    )(coords, intensity[None], start)


def cost(elements):
    return pl.CostEstimate(flops=40 * elements, bytes_accessed=2 * elements, transcendentals=2 * elements)


def near_kernel(count, feats_ref, *refs):
    packed_refs, (rows_ref, row_logs_ref, columns_ref, logs_ref, cov_ref, part_ref) = refs[:count], refs[count:]
    size, points = part_ref.shape
    rows, row_log = row_features(feats_ref[...].astype(F32))
    rows_ref[...], row_logs_ref[...] = rows, row_log
    made = [column_features(ref[...].astype(F32)[size:]) for ref in packed_refs]
    total = jnp.zeros(part_ref.shape, F32)
    for c, ref in enumerate(packed_refs):
        to = slice(c * points, (c + 1) * points)
        columns_ref[:, to], logs_ref[:, to] = made[c]
        cov_ref[:, to] = tile_of(rows, row_log, *made[c])
        total += lax.dot_general(ref[:size], cov_ref[:, to], NT, preferred_element_type=F32)
    part_ref[...] = total


def near(feats, packed):
    rows, points = packed[0].shape
    total = len(packed) * points
    return pl.pallas_call(
        functools.partial(near_kernel, len(packed)),
        out_shape=(
            pltpu.VMEM((points, DEPTH), BF16),
            pltpu.VMEM((points, LANES), F32),
            pltpu.VMEM((DEPTH, total), BF16),
            pltpu.VMEM((1, total), F32),
            pltpu.VMEM((points, total), BF16),
            pltpu.VMEM((rows - FEATS, points), F32),
        ),
        compiler_params=PARAMS,
        cost_estimate=cost(total * points),
        name="near",
    )(feats, *packed)


def far_kernel(count, near_ref, rows_ref, row_logs_ref, columns_ref, logs_ref, last_ref, *refs):
    feats_refs, packed_refs, (edge_ref, cov_ref, sum_ref, sent_ref) = refs[:count], refs[count:-4], refs[-4:]
    size, points = near_ref.shape
    made = [row_features(ref[...].astype(F32)) for ref in feats_refs]
    columns, logs = [], []
    for c in range(len(packed_refs)):
        to = slice(c * points, (c + 1) * points)
        columns.append(columns_ref[:, to])
        logs.append(logs_ref[:, to])
    last, last_log = column_features(last_ref[...].astype(F32)[size:])
    columns.append(last)
    logs.append(last_log)
    sources = list(packed_refs) + [last_ref]
    edge_ref[...] = tile_of(rows_ref[...], row_logs_ref[...], last, last_log)
    total = near_ref[...] + lax.dot_general(last_ref[:size], edge_ref[...], NT, preferred_element_type=F32)
    sum_ref[0] = total
    sent_ref[0] = total.astype(BF16)
    for k in range(count):
        at = slice(k * points, (k + 1) * points)
        total = jnp.zeros(near_ref.shape, F32)
        for c, ref in enumerate(sources):
            to = slice(c * points, (c + 1) * points)
            cov_ref[at, to] = tile_of(*made[k], columns[c], logs[c])
            total += lax.dot_general(ref[:size], cov_ref[at, to], NT, preferred_element_type=F32)
        sum_ref[k + 1] = total
        sent_ref[k + 1] = total.astype(BF16)


def far(near_part, rows, row_logs, columns, logs, feats, packed, last):
    size, points = near_part.shape
    height, wide = len(feats) * points, (len(packed) + 1) * points
    return pl.pallas_call(
        functools.partial(far_kernel, len(feats)),
        out_shape=(
            pltpu.VMEM((points, points), BF16),
            pltpu.VMEM((height, wide), BF16),
            pltpu.VMEM((1 + len(feats), size, points), F32),
            pltpu.VMEM((1 + len(feats), size, points), BF16),
        ),
        compiler_params=PARAMS,
        cost_estimate=cost((height + points) * wide),
        name="far",
    )(near_part, rows, row_logs, columns, logs, last, *feats, *packed)


def gram_of(product):
    return lax.dot_general(product, product, NT, precision=lax.Precision.HIGHEST, preferred_element_type=F32)


def fold(second_gram, first_gram):
    half = second_gram.shape[0] // 2
    both = jnp.concatenate([second_gram, first_gram], axis=1)
    return jnp.concatenate([both[:half], both[half:]], axis=1)


def unfold(folded):
    size = 2 * folded.shape[0]
    both = jnp.concatenate([folded[:, : 2 * size], folded[:, 2 * size :]], axis=0)
    return both[:, :size], both[:, size:]


def second_kernel(own_ref, *refs):
    part_refs, near_ref, edge_ref, far_ref, outs, gram_ref = refs[:3], refs[3], refs[4], refs[5], refs[6:-1], refs[-1]
    count, size, points = own_ref.shape
    totals = [jnp.zeros((2 * size, points), F32) for _ in outs]
    for k in range(count):
        a, b, c = (ref[k ^ (n + 1)].astype(F32) for n, ref in enumerate(part_refs))
        product = (own_ref[k] + a) + (b + c)
        if k == 0:
            gram_ref[...] = gram_of(product)
        vectors = jnp.concatenate(split(product, 2), axis=0).astype(BF16)
        for n in range(len(outs)):
            to = slice(n * points, (n + 1) * points)
            if k == 0:
                cov = near_ref[:, to] if n < len(outs) - 1 else edge_ref[...]
            else:
                cov = far_ref[(k - 1) * points : k * points, to]
            totals[n] += jnp.dot(vectors, cov, preferred_element_type=F32)
    for ref, total in zip(outs, totals):
        ref[...] = total[:size] + total[size:]


def second(own, parts, near_cov, edge_cov, far_cov):
    _, size, points = own.shape
    blocks = far_cov.shape[1] // points
    return pl.pallas_call(
        second_kernel,
        out_shape=[pltpu.VMEM((size, points), F32)] * blocks + [pltpu.VMEM((size, size), F32)],
        compiler_params=PARAMS,
        name="second",
    )(own, *parts, near_cov, edge_cov, far_cov)


def gather_kernel(first_ref, own_ref, *refs):
    part_refs, (product_ref, gram_ref) = refs[:-2], refs[-2:]
    product = own_ref[...]
    for ref in part_refs:
        product += ref[...]
    product_ref[...] = product
    gram_ref[...] = fold(gram_of(product), first_ref[...])


def gather_parts(first_gram, own, parts):
    size, points = own.shape
    return pl.pallas_call(
        gather_kernel,
        out_shape=(pltpu.VMEM((size, points), F32), pltpu.VMEM((size // 2, 4 * size), F32)),
        compiler_params=SMALL,
        name="gather_parts",
    )(first_gram, own, *parts)


def row_kernel(packed_ref, feats_ref, out_ref):
    size = out_ref.shape[0]
    rows, row_log = row_features(feats_ref[...].astype(F32))
    out_ref[...] = jnp.zeros(out_ref.shape, F32)

    def step(k, carry):
        packed = packed_ref[k]
        columns, column_log = column_features(packed[size:].astype(F32))
        tile = tile_of(rows, row_log, columns, column_log)
        out_ref[...] += lax.dot_general(packed[:size], tile, NT, preferred_element_type=F32)
        return carry

    lax.fori_loop(0, packed_ref.shape[0], step, 0)


def row_product(packed, feats):
    _, rows, points = packed.shape
    return pl.pallas_call(
        row_kernel,
        out_shape=jax.ShapeDtypeStruct((rows - FEATS, points), F32),
        compiler_params=PARAMS,
        name="row_product",
    )(packed, feats)


def grams_kernel(second_ref, first_ref, gram_ref):
    gram_ref[...] = fold(gram_of(second_ref[...]), gram_of(first_ref[...]))


def grams(second_product, first_product):
    size = first_product.shape[0]
    return pl.pallas_call(
        grams_kernel,
        out_shape=jax.ShapeDtypeStruct((size // 2, 4 * size), F32),
        compiler_params=SMALL,
        name="grams",
    )(second_product, first_product)


def eliminate(gram):
    size = gram.shape[0]
    wide = (size, LANES)
    index = row_of(wide)
    cols = [jnp.broadcast_to(gram[:, k : k + 1], wide) for k in range(size)]
    multipliers, factor_cols = [], []
    scale = jnp.zeros(wide, F32)
    for k in range(size):
        pivot = jnp.broadcast_to(cols[k][k : k + 1], wide)
        root = 1.0 / jnp.sqrt(pivot)
        multiplier = jnp.where(index > k, cols[k] / pivot, 0.0)
        for j in range(k + 1, size):
            cols[j] = cols[j] - multiplier * jnp.broadcast_to(cols[j][k : k + 1], wide)
        multipliers.append(multiplier)
        factor_cols.append(jnp.where(index >= k, cols[k] * root, 0.0))
        scale = jnp.where(index == k, root, scale)
    return multipliers, factor_cols, scale


def finish_kernel(total_points, product_ref, *refs):
    gram_refs, (basis_ref, factor_ref) = refs[:-2], refs[-2:]
    size, points = product_ref.shape
    gram = gram_refs[0][...] + gram_refs[1][...]
    if len(gram_refs) > 2:
        gram = gram + (gram_refs[2][...] + gram_refs[3][...])
    gram, first_gram = unfold(gram / total_points)
    steps, cols, scale = eliminate(gram)
    first_steps, _, first_scale = eliminate(first_gram)
    for at in range(0, points, LANES):
        part = product_ref[:, at : at + LANES]
        for k in range(size):
            part = part - steps[k] * part[k : k + 1]
        basis_ref[:, at : at + LANES] = part * scale
    lane = lax.broadcasted_iota(jnp.int32, (size, LANES), 1)
    factor = jnp.zeros((size, LANES), F32)
    for k in range(size):
        factor = jnp.where(lane == k, cols[k], factor)
    for k in range(size):
        factor = factor - first_steps[k] * factor[k : k + 1]
    factor_ref[...] = (factor * first_scale)[:, :size]


def finish(product, gram_parts, total_points):
    size, points = product.shape
    return pl.pallas_call(
        functools.partial(finish_kernel, total_points),
        out_shape=(jax.ShapeDtypeStruct((size, points), F32), jax.ShapeDtypeStruct((size, size), F32)),
        compiler_params=SMALL,
        name="finish",
    )(product, *gram_parts)


def rounds_of(width):
    bits = [1 << k for k in range(width.bit_length() - 1)][::-1]
    out = []
    while bits:
        take = 1 if len(bits) % 2 else 2
        group, bits = bits[:take], bits[take:]
        out.append([group[0]] if take == 1 else [group[1], group[0], group[0] + group[1]])
    return out


def exchange(value, distance, width):
    return lax.ppermute(value, "wide", [(k, k ^ distance) for k in range(width)])


def sum_parts(value, width):
    rounds = rounds_of(width)[::-1]
    rounds = rounds[:1] + [[d + 1 if d.bit_count() == 1 else d ^ 1 for d in r] for r in rounds[1:]]
    for n, distances in enumerate(rounds):
        parts = [value] + [exchange(value, d, width) for d in distances]
        if n == len(rounds) - 1:
            return parts
        value = parts[1] + parts[0]
        if len(parts) > 2:
            value = value + (parts[3] + parts[2])


def gather_blocks(value, width):
    held = value[None]
    for distances in rounds_of(width):
        held = jnp.concatenate([held] + [exchange(held, d, width) for d in distances], axis=0)
    return held


def body(coords, intensity, start):
    width = lax.axis_size("wide")
    size, points = start.shape
    packed, feats = prepare(coords, intensity, start)
    if width == 16:
        near_steps, far_steps = (1, 2, 3), (8, 13, 5)
        blocks = [packed] + [exchange(packed, d, width) for d in far_steps]
        others = [exchange(feats, d, width) for d in near_steps]
        *features, near_cov, part = near(feats, blocks[:-1])
        edge_cov, far_cov, own, sent = far(part, *features, others, blocks[:-1], blocks[-1])
        parts = [exchange(own if d == 1 else sent, d, width) for d in near_steps]
        *products, first_gram = second(own, parts, near_cov, edge_cov, far_cov)
        got = [exchange(p, d, width) for p, d in zip(products[1:], far_steps)]
        product, gram = gather_parts(first_gram, products[0], got)
    else:
        everything = gather_blocks(packed, width)
        first_product = row_product(everything, feats)
        vectors = gather_blocks(first_product.astype(BF16), width)
        product = row_product(jnp.concatenate([vectors, everything[:, size:]], axis=1), feats)
        gram = grams(product, first_product)
    return finish(product, sum_parts(gram, width), float(points * width))


def solution(mesh):
    placed = (P(None, ("camp", "wide")), P(("camp", "wide")), P(None, ("camp", "wide")))
    return jax.shard_map(
        body,
        mesh=mesh,
        in_specs=placed,
        out_specs=(P(None, ("camp", "wide")), P("camp", None)),
        check_vma=False,
    )
```

```python
import functools
import math

import jax
import jax.numpy as jnp
from jax import lax
from jax.experimental import pallas as pl
from jax.experimental.pallas import tpu as pltpu
from jax.sharding import PartitionSpec as P

LOG2E = 1.0 / math.log(2.0)
SCALE = 3.0**0.5 / 0.15 * LOG2E
LOG2_LN2 = math.log2(math.log(2.0))
SMALLEST = 1e-4
FEATS = 8
DEPTH = 4 * FEATS
LANES = 128
F32, BF16 = jnp.float32, jnp.bfloat16
NT = (((1,), (1,)), ((), ()))
PARAMS = pltpu.CompilerParams(vmem_limit_bytes=24 * 2**20)
SMALL = pltpu.CompilerParams(vmem_limit_bytes=8 * 2**20)


def split(value, parts):
    out = []
    for _ in range(parts):
        part = value.astype(BF16).astype(F32)
        out.append(part)
        value = value - part
    return out


def row_of(shape):
    return lax.broadcasted_iota(jnp.int32, shape, 0)


def stack_rows(rows, shape):
    index = row_of(shape)
    out = jnp.zeros(shape, F32)
    for k, row in rows.items():
        out = jnp.where(index == k, row, out)
    return out


def norms(feats):
    whole = feats + jnp.roll(feats, -3, axis=0)
    squares = jnp.where(row_of(feats.shape) < 3, whole * whole, 0.0)
    return split(jnp.sum(squares, axis=0, keepdims=True), 3)


def row_features(feats):
    shape = feats.shape
    n1, n2, n3 = norms(feats)
    p1, p2, p3 = split(feats[6:7] + feats[7:8] + LOG2_LN2, 3)
    index = row_of(shape)
    double = -2.0 * feats
    with_hi = jnp.where(index < 3, double, jnp.where(index < 6, jnp.roll(double, 3, axis=0), 0.0))
    with_lo = jnp.where(index < 3, jnp.roll(double, -3, axis=0), jnp.where(index < 6, double, 0.0))
    with_norm = stack_rows({0: 1.0, 1: 1.0, 2: 1.0, 3: n1, 4: n2, 5: n3}, shape)
    with_log = stack_rows({0: p1, 1: p2, 2: p3}, shape)
    rows = jnp.swapaxes(jnp.concatenate([with_hi, with_lo, with_norm, with_log], axis=0), 0, 1).astype(BF16)
    index = row_of((DEPTH, LANES))
    pick = jnp.where((index >= 3 * FEATS) & (index < 3 * FEATS + 3), 1.0, 0.0).astype(BF16)
    return rows, jnp.dot(rows, pick, preferred_element_type=F32)


def column_features(feats):
    n1, n2, n3 = norms(feats)
    with_norm = stack_rows({0: n1, 1: n2, 2: n3, 3: 1.0, 4: 1.0, 5: 1.0}, feats.shape)
    columns = jnp.concatenate([feats, feats, with_norm, jnp.zeros(feats.shape, F32)], axis=0).astype(BF16)
    return columns, feats[6:7] + feats[7:8]


def tile_of(rows, row_log, columns, column_log):
    points = columns.shape[1]
    squared = jnp.dot(rows, columns, preferred_element_type=F32)
    scaled = squared * lax.rsqrt(jnp.maximum(squared, SMALLEST))
    logs = jnp.concatenate([row_log] * (points // LANES), axis=1) + column_log
    return ((scaled + LOG2E) * jnp.exp2(logs - scaled)).astype(BF16)


def prepare_kernel(*refs):
    sources, (packed_ref, feats_ref), buffers, sems = refs[:3], refs[3:5], refs[5:8], refs[8]
    copies = [pltpu.make_async_copy(a, b, sems.at[n]) for n, (a, b) in enumerate(zip(sources, buffers))]
    for copy in copies:
        copy.start()
    for copy in copies:
        copy.wait()
    coords_ref, intensity_ref, start_ref = buffers
    hi, lo = split((coords_ref[...] - 0.5) * SCALE, 2)
    log_hi, log_lo = split(jnp.log2(intensity_ref[...]), 2)
    rows = {k: hi[k : k + 1] for k in range(3)}
    rows.update({3 + k: lo[k : k + 1] for k in range(3)})
    rows.update({6: log_hi, 7: log_lo})
    feats = stack_rows(rows, feats_ref.shape)
    packed_ref[...] = jnp.concatenate([start_ref[...].astype(F32), feats], axis=0).astype(BF16)
    feats_ref[...] = feats.astype(BF16)


def prepare(coords, intensity, start):
    columns, points = start.shape
    return pl.pallas_call(
        prepare_kernel,
        in_specs=[pl.BlockSpec(memory_space=pltpu.HBM)] * 3,
        out_shape=(pltpu.VMEM((columns + FEATS, points), BF16), pltpu.VMEM((FEATS, points), BF16)),
        scratch_shapes=[
            pltpu.VMEM(coords.shape, F32),
            pltpu.VMEM((1, points), F32),
            pltpu.VMEM(start.shape, BF16),
            pltpu.SemaphoreType.DMA((3,)),
        ],
        name="prepare",
    )(coords, intensity[None], start)


def cost(elements):
    return pl.CostEstimate(flops=40 * elements, bytes_accessed=2 * elements, transcendentals=2 * elements)


def near_kernel(count, feats_ref, *refs):
    packed_refs, (rows_ref, row_logs_ref, columns_ref, logs_ref, cov_ref, part_ref) = refs[:count], refs[count:]
    size, points = part_ref.shape
    rows, row_log = row_features(feats_ref[...].astype(F32))
    rows_ref[...], row_logs_ref[...] = rows, row_log
    made = [column_features(ref[...].astype(F32)[size:]) for ref in packed_refs]
    total = jnp.zeros(part_ref.shape, F32)
    for c, ref in enumerate(packed_refs):
        to = slice(c * points, (c + 1) * points)
        columns_ref[:, to], logs_ref[:, to] = made[c]
        cov_ref[:, to] = tile_of(rows, row_log, *made[c])
        total += lax.dot_general(ref[:size], cov_ref[:, to], NT, preferred_element_type=F32)
    part_ref[...] = total


def near(feats, packed):
    rows, points = packed[0].shape
    total = len(packed) * points
    return pl.pallas_call(
        functools.partial(near_kernel, len(packed)),
        out_shape=(
            pltpu.VMEM((points, DEPTH), BF16),
            pltpu.VMEM((points, LANES), F32),
            pltpu.VMEM((DEPTH, total), BF16),
            pltpu.VMEM((1, total), F32),
            pltpu.VMEM((points, total), BF16),
            pltpu.VMEM((rows - FEATS, points), F32),
        ),
        compiler_params=PARAMS,
        cost_estimate=cost(total * points),
        name="near",
    )(feats, *packed)


def far_kernel(count, near_ref, rows_ref, row_logs_ref, columns_ref, logs_ref, last_ref, *refs):
    feats_refs, packed_refs, (edge_ref, cov_ref, sum_ref, sent_ref) = refs[:count], refs[count:-4], refs[-4:]
    size, points = near_ref.shape
    made = [row_features(ref[...].astype(F32)) for ref in feats_refs]
    columns, logs = [], []
    for c in range(len(packed_refs)):
        to = slice(c * points, (c + 1) * points)
        columns.append(columns_ref[:, to])
        logs.append(logs_ref[:, to])
    last, last_log = column_features(last_ref[...].astype(F32)[size:])
    columns.append(last)
    logs.append(last_log)
    sources = list(packed_refs) + [last_ref]
    edge_ref[...] = tile_of(rows_ref[...], row_logs_ref[...], last, last_log)
    total = near_ref[...] + lax.dot_general(last_ref[:size], edge_ref[...], NT, preferred_element_type=F32)
    sum_ref[0] = total
    sent_ref[0] = total.astype(BF16)
    for k in range(count):
        at = slice(k * points, (k + 1) * points)
        total = jnp.zeros(near_ref.shape, F32)
        for c, ref in enumerate(sources):
            to = slice(c * points, (c + 1) * points)
            cov_ref[at, to] = tile_of(*made[k], columns[c], logs[c])
            total += lax.dot_general(ref[:size], cov_ref[at, to], NT, preferred_element_type=F32)
        sum_ref[k + 1] = total
        sent_ref[k + 1] = total.astype(BF16)


def far(near_part, rows, row_logs, columns, logs, feats, packed, last):
    size, points = near_part.shape
    height, wide = len(feats) * points, (len(packed) + 1) * points
    return pl.pallas_call(
        functools.partial(far_kernel, len(feats)),
        out_shape=(
            pltpu.VMEM((points, points), BF16),
            pltpu.VMEM((height, wide), BF16),
            pltpu.VMEM((1 + len(feats), size, points), F32),
            pltpu.VMEM((1 + len(feats), size, points), BF16),
        ),
        compiler_params=PARAMS,
        cost_estimate=cost((height + points) * wide),
        name="far",
    )(near_part, rows, row_logs, columns, logs, last, *feats, *packed)


def gram_of(product):
    return lax.dot_general(product, product, NT, precision=lax.Precision.HIGHEST, preferred_element_type=F32)


def fold(second_gram, first_gram):
    half = second_gram.shape[0] // 2
    both = jnp.concatenate([second_gram, first_gram], axis=1)
    return jnp.concatenate([both[:half], both[half:]], axis=1)


def unfold(folded):
    size = 2 * folded.shape[0]
    both = jnp.concatenate([folded[:, : 2 * size], folded[:, 2 * size :]], axis=0)
    return both[:, :size], both[:, size:]


def second_kernel(own_ref, *refs):
    part_refs, near_ref, edge_ref, far_ref, outs = refs[:3], refs[3], refs[4], refs[5], refs[6:-2]
    vectors_ref, first_ref = refs[-2:]
    count, size, points = own_ref.shape
    last = len(outs)
    totals = [jnp.zeros((2 * size, points), F32) for _ in outs]
    for k in range(count):
        a, b, c = (ref[k ^ (n + 1)].astype(F32) for n, ref in enumerate(part_refs))
        product = (own_ref[k] + a) + (b + c)
        if k == 0:
            first_ref[...] = product
        vectors = jnp.concatenate(split(product, 2), axis=0).astype(BF16)
        vectors_ref[k] = vectors
        for n in range(1, last + 1):
            to = slice(n * points, (n + 1) * points)
            if k == 0:
                cov = near_ref[:, to] if n < last else edge_ref[...]
            else:
                cov = far_ref[(k - 1) * points : k * points, to]
            totals[n - 1] += jnp.dot(vectors, cov, preferred_element_type=F32)
    for ref, total in zip(outs, totals):
        ref[...] = total[:size] + total[size:]


def second(own, parts, near_cov, edge_cov, far_cov):
    count, size, points = own.shape
    others = far_cov.shape[1] // points - 1
    return pl.pallas_call(
        second_kernel,
        out_shape=[pltpu.VMEM((size, points), F32)] * others
        + [pltpu.VMEM((count, 2 * size, points), BF16), pltpu.VMEM((size, points), F32)],
        compiler_params=PARAMS,
        cost_estimate=cost(count * points * others * points // 8),
        name="second",
    )(own, *parts, near_cov, edge_cov, far_cov)


def kept_kernel(vectors_ref, first_ref, near_ref, far_ref, out_ref, gram_ref):
    count, double, points = vectors_ref.shape
    total = jnp.dot(vectors_ref[0], near_ref[:, :points], preferred_element_type=F32)
    for k in range(1, count):
        cov = far_ref[(k - 1) * points : k * points, :points]
        total += jnp.dot(vectors_ref[k], cov, preferred_element_type=F32)
    out_ref[...] = total[: double // 2] + total[double // 2 :]
    gram_ref[...] = gram_of(first_ref[...])


def kept(vectors, first, near_cov, far_cov):
    size, points = first.shape
    return pl.pallas_call(
        kept_kernel,
        out_shape=(pltpu.VMEM((size, points), F32), pltpu.VMEM((size, size), F32)),
        compiler_params=PARAMS,
        cost_estimate=cost(vectors.shape[0] * points * points // 8),
        name="kept",
    )(vectors, first, near_cov, far_cov)


def gather_kernel(first_ref, own_ref, *refs):
    part_refs, (product_ref, gram_ref) = refs[:-2], refs[-2:]
    product = own_ref[...]
    for ref in part_refs:
        product += ref[...]
    product_ref[...] = product
    gram_ref[...] = fold(gram_of(product), first_ref[...])


def gather_parts(first_gram, own, parts):
    size, points = own.shape
    return pl.pallas_call(
        gather_kernel,
        out_shape=(pltpu.VMEM((size, points), F32), pltpu.VMEM((size // 2, 4 * size), F32)),
        compiler_params=SMALL,
        name="gather_parts",
    )(first_gram, own, *parts)


def row_kernel(packed_ref, feats_ref, out_ref):
    size = out_ref.shape[0]
    rows, row_log = row_features(feats_ref[...].astype(F32))
    out_ref[...] = jnp.zeros(out_ref.shape, F32)

    def step(k, carry):
        packed = packed_ref[k]
        columns, column_log = column_features(packed[size:].astype(F32))
        tile = tile_of(rows, row_log, columns, column_log)
        out_ref[...] += lax.dot_general(packed[:size], tile, NT, preferred_element_type=F32)
        return carry

    lax.fori_loop(0, packed_ref.shape[0], step, 0)


def row_product(packed, feats):
    _, rows, points = packed.shape
    return pl.pallas_call(
        row_kernel,
        out_shape=jax.ShapeDtypeStruct((rows - FEATS, points), F32),
        compiler_params=PARAMS,
        name="row_product",
    )(packed, feats)


def grams_kernel(second_ref, first_ref, gram_ref):
    gram_ref[...] = fold(gram_of(second_ref[...]), gram_of(first_ref[...]))


def grams(second_product, first_product):
    size = first_product.shape[0]
    return pl.pallas_call(
        grams_kernel,
        out_shape=jax.ShapeDtypeStruct((size // 2, 4 * size), F32),
        compiler_params=SMALL,
        name="grams",
    )(second_product, first_product)


def eliminate(gram):
    size = gram.shape[0]
    wide = (size, LANES)
    index = row_of(wide)
    cols = [jnp.broadcast_to(gram[:, k : k + 1], wide) for k in range(size)]
    multipliers, factor_cols = [], []
    scale = jnp.zeros(wide, F32)
    for k in range(size):
        pivot = jnp.broadcast_to(cols[k][k : k + 1], wide)
        root = 1.0 / jnp.sqrt(pivot)
        multiplier = jnp.where(index > k, cols[k] / pivot, 0.0)
        for j in range(k + 1, size):
            cols[j] = cols[j] - multiplier * jnp.broadcast_to(cols[j][k : k + 1], wide)
        multipliers.append(multiplier)
        factor_cols.append(jnp.where(index >= k, cols[k] * root, 0.0))
        scale = jnp.where(index == k, root, scale)
    return multipliers, factor_cols, scale


def finish_kernel(total_points, product_ref, *refs):
    gram_refs, (basis_ref, factor_ref) = refs[:-2], refs[-2:]
    size, points = product_ref.shape
    gram = gram_refs[0][...] + gram_refs[1][...]
    if len(gram_refs) > 2:
        gram = gram + (gram_refs[2][...] + gram_refs[3][...])
    gram, first_gram = unfold(gram / total_points)
    steps, cols, scale = eliminate(gram)
    first_steps, _, first_scale = eliminate(first_gram)
    for at in range(0, points, LANES):
        part = product_ref[:, at : at + LANES]
        for k in range(size):
            part = part - steps[k] * part[k : k + 1]
        basis_ref[:, at : at + LANES] = part * scale
    lane = lax.broadcasted_iota(jnp.int32, (size, LANES), 1)
    factor = jnp.zeros((size, LANES), F32)
    for k in range(size):
        factor = jnp.where(lane == k, cols[k], factor)
    for k in range(size):
        factor = factor - first_steps[k] * factor[k : k + 1]
    factor_ref[...] = (factor * first_scale)[:, :size]


def finish(product, gram_parts, total_points):
    size, points = product.shape
    return pl.pallas_call(
        functools.partial(finish_kernel, total_points),
        out_shape=(jax.ShapeDtypeStruct((size, points), F32), jax.ShapeDtypeStruct((size, size), F32)),
        compiler_params=SMALL,
        name="finish",
    )(product, *gram_parts)


def rounds_of(width):
    bits = [1 << k for k in range(width.bit_length() - 1)][::-1]
    out = []
    while bits:
        take = 1 if len(bits) % 2 else 2
        group, bits = bits[:take], bits[take:]
        out.append([group[0]] if take == 1 else [group[1], group[0], group[0] + group[1]])
    return out


def exchange(value, distance, width):
    return lax.ppermute(value, "wide", [(k, k ^ distance) for k in range(width)])


def sum_parts(value, width):
    rounds = rounds_of(width)[::-1]
    rounds = rounds[:1] + [[d + 1 if d.bit_count() == 1 else d ^ 1 for d in r] for r in rounds[1:]]
    for n, distances in enumerate(rounds):
        parts = [value] + [exchange(value, d, width) for d in distances]
        if n == len(rounds) - 1:
            return parts
        value = parts[1] + parts[0]
        if len(parts) > 2:
            value = value + (parts[3] + parts[2])


def gather_blocks(value, width):
    held = value[None]
    for distances in rounds_of(width):
        held = jnp.concatenate([held] + [exchange(held, d, width) for d in distances], axis=0)
    return held


def body(coords, intensity, start):
    width = lax.axis_size("wide")
    size, points = start.shape
    packed, feats = prepare(coords, intensity, start)
    if width == 16:
        near_steps, far_steps = (1, 2, 3), (13, 4, 9)
        blocks = [packed] + [exchange(packed, d, width) for d in far_steps]
        others = [exchange(feats, d, width) for d in near_steps]
        *features, near_cov, part = near(feats, blocks[:-1])
        edge_cov, far_cov, own, sent = far(part, *features, others, blocks[:-1], blocks[-1])
        parts = [exchange(own if d == 1 else sent, d, width) for d in near_steps]
        *products, vectors, first = second(own, parts, near_cov, edge_cov, far_cov)
        got = [exchange(p, d, width) for p, d in zip(products, far_steps)]
        product, first_gram = kept(vectors, first, near_cov, far_cov)
        product, gram = gather_parts(first_gram, product, got)
    else:
        everything = gather_blocks(packed, width)
        first_product = row_product(everything, feats)
        vectors = gather_blocks(first_product.astype(BF16), width)
        product = row_product(jnp.concatenate([vectors, everything[:, size:]], axis=1), feats)
        gram = grams(product, first_product)
    return finish(product, sum_parts(gram, width), float(points * width))


def solution(mesh):
    placed = (P(None, ("camp", "wide")), P(("camp", "wide")), P(None, ("camp", "wide")))
    return jax.shard_map(
        body,
        mesh=mesh,
        in_specs=placed,
        out_specs=(P(None, ("camp", "wide")), P("camp", None)),
        check_vma=False,
    )
```

```python
import functools
import math

import jax
import jax.numpy as jnp
from jax import lax
from jax.experimental import pallas as pl
from jax.experimental.pallas import tpu as pltpu
from jax.sharding import PartitionSpec as P

LOG2E = 1.0 / math.log(2.0)
SCALE = 3.0**0.5 / 0.15 * LOG2E
LOG2_LN2 = math.log2(math.log(2.0))
SMALLEST = 1e-4
FEATS = 8
DEPTH = 4 * FEATS
LANES = 128
F32, BF16 = jnp.float32, jnp.bfloat16
NT = (((1,), (1,)), ((), ()))
PARAMS = pltpu.CompilerParams(vmem_limit_bytes=24 * 2**20)
SMALL = pltpu.CompilerParams(vmem_limit_bytes=8 * 2**20)


def split(value, parts):
    out = []
    for _ in range(parts):
        part = value.astype(BF16).astype(F32)
        out.append(part)
        value = value - part
    return out


def row_of(shape):
    return lax.broadcasted_iota(jnp.int32, shape, 0)


def stack_rows(rows, shape):
    index = row_of(shape)
    out = jnp.zeros(shape, F32)
    for k, row in rows.items():
        out = jnp.where(index == k, row, out)
    return out


def norms(feats):
    whole = feats + jnp.roll(feats, -3, axis=0)
    squares = jnp.where(row_of(feats.shape) < 3, whole * whole, 0.0)
    return split(jnp.sum(squares, axis=0, keepdims=True), 3)


def row_features(feats):
    shape = feats.shape
    n1, n2, n3 = norms(feats)
    p1, p2, p3 = split(feats[6:7] + feats[7:8] + LOG2_LN2, 3)
    index = row_of(shape)
    double = -2.0 * feats
    with_hi = jnp.where(index < 3, double, jnp.where(index < 6, jnp.roll(double, 3, axis=0), 0.0))
    with_lo = jnp.where(index < 3, jnp.roll(double, -3, axis=0), jnp.where(index < 6, double, 0.0))
    with_norm = stack_rows({0: 1.0, 1: 1.0, 2: 1.0, 3: n1, 4: n2, 5: n3}, shape)
    with_log = stack_rows({0: p1, 1: p2, 2: p3}, shape)
    rows = jnp.swapaxes(jnp.concatenate([with_hi, with_lo, with_norm, with_log], axis=0), 0, 1).astype(BF16)
    index = row_of((DEPTH, LANES))
    pick = jnp.where((index >= 3 * FEATS) & (index < 3 * FEATS + 3), 1.0, 0.0).astype(BF16)
    return rows, jnp.dot(rows, pick, preferred_element_type=F32)


def column_features(feats):
    n1, n2, n3 = norms(feats)
    with_norm = stack_rows({0: n1, 1: n2, 2: n3, 3: 1.0, 4: 1.0, 5: 1.0}, feats.shape)
    columns = jnp.concatenate([feats, feats, with_norm, jnp.zeros(feats.shape, F32)], axis=0).astype(BF16)
    return columns, feats[6:7] + feats[7:8]


def tile_of(rows, row_log, columns, column_log):
    points = columns.shape[1]
    squared = jnp.dot(rows, columns, preferred_element_type=F32)
    scaled = squared * lax.rsqrt(jnp.maximum(squared, SMALLEST))
    logs = jnp.concatenate([row_log] * (points // LANES), axis=1) + column_log
    return ((scaled + LOG2E) * jnp.exp2(logs - scaled)).astype(BF16)


def prepare_kernel(*refs):
    sources, (packed_ref, feats_ref), buffers, sems = refs[:3], refs[3:5], refs[5:8], refs[8]
    copies = [pltpu.make_async_copy(a, b, sems.at[n]) for n, (a, b) in enumerate(zip(sources, buffers))]
    for copy in copies:
        copy.start()
    for copy in copies:
        copy.wait()
    coords_ref, intensity_ref, start_ref = buffers
    hi, lo = split((coords_ref[...] - 0.5) * SCALE, 2)
    log_hi, log_lo = split(jnp.log2(intensity_ref[...]), 2)
    rows = {k: hi[k : k + 1] for k in range(3)}
    rows.update({3 + k: lo[k : k + 1] for k in range(3)})
    rows.update({6: log_hi, 7: log_lo})
    feats = stack_rows(rows, feats_ref.shape)
    packed_ref[...] = jnp.concatenate([start_ref[...].astype(F32), feats], axis=0).astype(BF16)
    feats_ref[...] = feats.astype(BF16)


def prepare(coords, intensity, start):
    columns, points = start.shape
    return pl.pallas_call(
        prepare_kernel,
        in_specs=[pl.BlockSpec(memory_space=pltpu.HBM)] * 3,
        out_shape=(pltpu.VMEM((columns + FEATS, points), BF16), pltpu.VMEM((FEATS, points), BF16)),
        scratch_shapes=[
            pltpu.VMEM(coords.shape, F32),
            pltpu.VMEM((1, points), F32),
            pltpu.VMEM(start.shape, BF16),
            pltpu.SemaphoreType.DMA((3,)),
        ],
        name="prepare",
    )(coords, intensity[None], start)


def cost(elements):
    return pl.CostEstimate(flops=40 * elements, bytes_accessed=2 * elements, transcendentals=2 * elements)


def near_kernel(count, feats_ref, *refs):
    packed_refs, (rows_ref, row_logs_ref, columns_ref, logs_ref, cov_ref, part_ref) = refs[:count], refs[count:]
    size, points = part_ref.shape
    rows, row_log = row_features(feats_ref[...].astype(F32))
    rows_ref[...], row_logs_ref[...] = rows, row_log
    made = [column_features(ref[...].astype(F32)[size:]) for ref in packed_refs]
    total = jnp.zeros(part_ref.shape, F32)
    for c, ref in enumerate(packed_refs):
        to = slice(c * points, (c + 1) * points)
        columns_ref[:, to], logs_ref[:, to] = made[c]
        cov_ref[:, to] = tile_of(rows, row_log, *made[c])
        total += lax.dot_general(ref[:size], cov_ref[:, to], NT, preferred_element_type=F32)
    part_ref[...] = total


def near(feats, packed):
    rows, points = packed[0].shape
    total = len(packed) * points
    return pl.pallas_call(
        functools.partial(near_kernel, len(packed)),
        out_shape=(
            pltpu.VMEM((points, DEPTH), BF16),
            pltpu.VMEM((points, LANES), F32),
            pltpu.VMEM((DEPTH, total), BF16),
            pltpu.VMEM((1, total), F32),
            pltpu.VMEM((points, total), BF16),
            pltpu.VMEM((rows - FEATS, points), F32),
        ),
        compiler_params=PARAMS,
        cost_estimate=cost(total * points),
        name="near",
    )(feats, *packed)


def far_kernel(count, near_ref, rows_ref, row_logs_ref, columns_ref, logs_ref, last_ref, *refs):
    feats_refs, packed_refs, (edge_ref, cov_ref, sum_ref, sent_ref) = refs[:count], refs[count:-4], refs[-4:]
    size, points = near_ref.shape
    made = [row_features(ref[...].astype(F32)) for ref in feats_refs]
    columns, logs = [], []
    for c in range(len(packed_refs)):
        to = slice(c * points, (c + 1) * points)
        columns.append(columns_ref[:, to])
        logs.append(logs_ref[:, to])
    last, last_log = column_features(last_ref[...].astype(F32)[size:])
    columns.append(last)
    logs.append(last_log)
    sources = list(packed_refs) + [last_ref]
    edge_ref[...] = tile_of(rows_ref[...], row_logs_ref[...], last, last_log)
    total = near_ref[...] + lax.dot_general(last_ref[:size], edge_ref[...], NT, preferred_element_type=F32)
    sum_ref[0] = total
    sent_ref[0] = total.astype(BF16)
    for k in range(count):
        at = slice(k * points, (k + 1) * points)
        total = jnp.zeros(near_ref.shape, F32)
        for c, ref in enumerate(sources):
            to = slice(c * points, (c + 1) * points)
            cov_ref[at, to] = tile_of(*made[k], columns[c], logs[c])
            total += lax.dot_general(ref[:size], cov_ref[at, to], NT, preferred_element_type=F32)
        sum_ref[k + 1] = total
        sent_ref[k + 1] = total.astype(BF16)


def far(near_part, rows, row_logs, columns, logs, feats, packed, last):
    size, points = near_part.shape
    height, wide = len(feats) * points, (len(packed) + 1) * points
    return pl.pallas_call(
        functools.partial(far_kernel, len(feats)),
        out_shape=(
            pltpu.VMEM((points, points), BF16),
            pltpu.VMEM((height, wide), BF16),
            pltpu.VMEM((1 + len(feats), size, points), F32),
            pltpu.VMEM((1 + len(feats), size, points), BF16),
        ),
        compiler_params=PARAMS,
        cost_estimate=cost((height + points) * wide),
        name="far",
    )(near_part, rows, row_logs, columns, logs, last, *feats, *packed)


def gram_of(product):
    return lax.dot_general(product, product, NT, precision=lax.Precision.HIGHEST, preferred_element_type=F32)


def fold(second_gram, first_gram):
    half = second_gram.shape[0] // 2
    both = jnp.concatenate([second_gram, first_gram], axis=1)
    return jnp.concatenate([both[:half], both[half:]], axis=1)


def unfold(folded):
    size = 2 * folded.shape[0]
    both = jnp.concatenate([folded[:, : 2 * size], folded[:, 2 * size :]], axis=0)
    return both[:, :size], both[:, size:]


def second_kernel(own_ref, *refs):
    part_refs, near_ref, edge_ref, far_ref, outs = refs[:3], refs[3], refs[4], refs[5], refs[6:-2]
    vectors_ref, first_ref = refs[-2:]
    count, size, points = own_ref.shape
    last = len(outs)
    totals = [jnp.zeros((size, points), F32) for _ in outs]
    for k in range(count):
        a, b, c = (ref[k ^ (n + 1)].astype(F32) for n, ref in enumerate(part_refs))
        product = (own_ref[k] + a) + (b + c)
        if k == 0:
            first_ref[...] = product
        vectors = product.astype(BF16)
        vectors_ref[k] = vectors
        for n in range(1, last + 1):
            to = slice(n * points, (n + 1) * points)
            if k == 0:
                cov = near_ref[:, to] if n < last else edge_ref[...]
            else:
                cov = far_ref[(k - 1) * points : k * points, to]
            totals[n - 1] += jnp.dot(vectors, cov, preferred_element_type=F32)
    for ref, total in zip(outs, totals):
        ref[...] = total


def second(own, parts, near_cov, edge_cov, far_cov):
    count, size, points = own.shape
    others = far_cov.shape[1] // points - 1
    return pl.pallas_call(
        second_kernel,
        out_shape=[pltpu.VMEM((size, points), F32)] * others
        + [pltpu.VMEM((count, size, points), BF16), pltpu.VMEM((size, points), F32)],
        compiler_params=PARAMS,
        cost_estimate=cost(count * points * others * points // 8),
        name="second",
    )(own, *parts, near_cov, edge_cov, far_cov)


def kept_kernel(vectors_ref, first_ref, near_ref, far_ref, out_ref, gram_ref):
    count, _, points = vectors_ref.shape
    total = jnp.dot(vectors_ref[0], near_ref[:, :points], preferred_element_type=F32)
    for k in range(1, count):
        cov = far_ref[(k - 1) * points : k * points, :points]
        total += jnp.dot(vectors_ref[k], cov, preferred_element_type=F32)
    out_ref[...] = total
    gram_ref[...] = gram_of(first_ref[...])


def kept(vectors, first, near_cov, far_cov):
    size, points = first.shape
    return pl.pallas_call(
        kept_kernel,
        out_shape=(pltpu.VMEM((size, points), F32), pltpu.VMEM((size, size), F32)),
        compiler_params=PARAMS,
        cost_estimate=cost(vectors.shape[0] * points * points // 8),
        name="kept",
    )(vectors, first, near_cov, far_cov)


def gather_kernel(first_ref, own_ref, *refs):
    part_refs, (product_ref, gram_ref) = refs[:-2], refs[-2:]
    product = own_ref[...]
    for ref in part_refs:
        product += ref[...]
    product_ref[...] = product
    gram_ref[...] = fold(gram_of(product), first_ref[...])


def gather_parts(first_gram, own, parts):
    size, points = own.shape
    return pl.pallas_call(
        gather_kernel,
        out_shape=(pltpu.VMEM((size, points), F32), pltpu.VMEM((size // 2, 4 * size), F32)),
        compiler_params=SMALL,
        name="gather_parts",
    )(first_gram, own, *parts)


def row_kernel(packed_ref, feats_ref, out_ref):
    size = out_ref.shape[0]
    rows, row_log = row_features(feats_ref[...].astype(F32))
    out_ref[...] = jnp.zeros(out_ref.shape, F32)

    def step(k, carry):
        packed = packed_ref[k]
        columns, column_log = column_features(packed[size:].astype(F32))
        tile = tile_of(rows, row_log, columns, column_log)
        out_ref[...] += lax.dot_general(packed[:size], tile, NT, preferred_element_type=F32)
        return carry

    lax.fori_loop(0, packed_ref.shape[0], step, 0)


def row_product(packed, feats):
    _, rows, points = packed.shape
    return pl.pallas_call(
        row_kernel,
        out_shape=jax.ShapeDtypeStruct((rows - FEATS, points), F32),
        compiler_params=PARAMS,
        name="row_product",
    )(packed, feats)


def grams_kernel(second_ref, first_ref, gram_ref):
    gram_ref[...] = fold(gram_of(second_ref[...]), gram_of(first_ref[...]))


def grams(second_product, first_product):
    size = first_product.shape[0]
    return pl.pallas_call(
        grams_kernel,
        out_shape=jax.ShapeDtypeStruct((size // 2, 4 * size), F32),
        compiler_params=SMALL,
        name="grams",
    )(second_product, first_product)


def eliminate(gram):
    size = gram.shape[0]
    wide = (size, LANES)
    index = row_of(wide)
    cols = [jnp.broadcast_to(gram[:, k : k + 1], wide) for k in range(size)]
    multipliers, factor_cols = [], []
    scale = jnp.zeros(wide, F32)
    for k in range(size):
        pivot = jnp.broadcast_to(cols[k][k : k + 1], wide)
        root = 1.0 / jnp.sqrt(pivot)
        multiplier = jnp.where(index > k, cols[k] / pivot, 0.0)
        for j in range(k + 1, size):
            cols[j] = cols[j] - multiplier * jnp.broadcast_to(cols[j][k : k + 1], wide)
        multipliers.append(multiplier)
        factor_cols.append(jnp.where(index >= k, cols[k] * root, 0.0))
        scale = jnp.where(index == k, root, scale)
    return multipliers, factor_cols, scale


def finish_kernel(total_points, product_ref, *refs):
    gram_refs, (basis_ref, factor_ref) = refs[:-2], refs[-2:]
    size, points = product_ref.shape
    gram = gram_refs[0][...] + gram_refs[1][...]
    if len(gram_refs) > 2:
        gram = gram + (gram_refs[2][...] + gram_refs[3][...])
    gram, first_gram = unfold(gram / total_points)
    steps, cols, scale = eliminate(gram)
    first_steps, _, first_scale = eliminate(first_gram)
    for at in range(0, points, LANES):
        part = product_ref[:, at : at + LANES]
        for k in range(size):
            part = part - steps[k] * part[k : k + 1]
        basis_ref[:, at : at + LANES] = part * scale
    lane = lax.broadcasted_iota(jnp.int32, (size, LANES), 1)
    factor = jnp.zeros((size, LANES), F32)
    for k in range(size):
        factor = jnp.where(lane == k, cols[k], factor)
    for k in range(size):
        factor = factor - first_steps[k] * factor[k : k + 1]
    factor_ref[...] = (factor * first_scale)[:, :size]


def finish(product, gram_parts, total_points):
    size, points = product.shape
    return pl.pallas_call(
        functools.partial(finish_kernel, total_points),
        out_shape=(jax.ShapeDtypeStruct((size, points), F32), jax.ShapeDtypeStruct((size, size), F32)),
        compiler_params=SMALL,
        name="finish",
    )(product, *gram_parts)


def rounds_of(width):
    bits = [1 << k for k in range(width.bit_length() - 1)][::-1]
    out = []
    while bits:
        take = 1 if len(bits) % 2 else 2
        group, bits = bits[:take], bits[take:]
        out.append([group[0]] if take == 1 else [group[1], group[0], group[0] + group[1]])
    return out


def exchange(value, distance, width):
    return lax.ppermute(value, "wide", [(k, k ^ distance) for k in range(width)])


def sum_parts(value, width):
    rounds = rounds_of(width)[::-1]
    rounds = rounds[:1] + [[d + 1 if d.bit_count() == 1 else d ^ 1 for d in r] for r in rounds[1:]]
    for n, distances in enumerate(rounds):
        parts = [value] + [exchange(value, d, width) for d in distances]
        if n == len(rounds) - 1:
            return parts
        value = parts[1] + parts[0]
        if len(parts) > 2:
            value = value + (parts[3] + parts[2])


def gather_blocks(value, width):
    held = value[None]
    for distances in rounds_of(width):
        held = jnp.concatenate([held] + [exchange(held, d, width) for d in distances], axis=0)
    return held


def body(coords, intensity, start):
    width = lax.axis_size("wide")
    size, points = start.shape
    packed, feats = prepare(coords, intensity, start)
    if width == 16:
        near_steps, far_steps = (1, 2, 3), (13, 4, 9)
        blocks = [packed] + [exchange(packed, d, width) for d in far_steps]
        others = [exchange(feats, d, width) for d in near_steps]
        *features, near_cov, part = near(feats, blocks[:-1])
        edge_cov, far_cov, own, sent = far(part, *features, others, blocks[:-1], blocks[-1])
        parts = [exchange(own if d == 1 else sent, d, width) for d in near_steps]
        *products, vectors, first = second(own, parts, near_cov, edge_cov, far_cov)
        got = [exchange(p, d, width) for p, d in zip(products, far_steps)]
        product, first_gram = kept(vectors, first, near_cov, far_cov)
        product, gram = gather_parts(first_gram, product, got)
    else:
        everything = gather_blocks(packed, width)
        first_product = row_product(everything, feats)
        vectors = gather_blocks(first_product.astype(BF16), width)
        product = row_product(jnp.concatenate([vectors, everything[:, size:]], axis=1), feats)
        gram = grams(product, first_product)
    return finish(product, sum_parts(gram, width), float(points * width))


def solution(mesh):
    placed = (P(None, ("camp", "wide")), P(("camp", "wide")), P(None, ("camp", "wide")))
    return jax.shard_map(
        body,
        mesh=mesh,
        in_specs=placed,
        out_specs=(P(None, ("camp", "wide")), P("camp", None)),
        check_vma=False,
    )
```

```python
import functools
import math

import jax
import jax.numpy as jnp
from jax import lax
from jax.experimental import pallas as pl
from jax.experimental.pallas import tpu as pltpu
from jax.sharding import PartitionSpec as P

LOG2E = 1.0 / math.log(2.0)
SCALE = 3.0**0.5 / 0.15 * LOG2E
LOG2_LN2 = math.log2(math.log(2.0))
SMALLEST = 1e-4
FEATS = 8
DEPTH = 4 * FEATS
LANES = 128
F32, BF16 = jnp.float32, jnp.bfloat16
NT = (((1,), (1,)), ((), ()))
PARAMS = pltpu.CompilerParams(vmem_limit_bytes=24 * 2**20)
SMALL = pltpu.CompilerParams(vmem_limit_bytes=8 * 2**20)


def split(value, parts):
    out = []
    for _ in range(parts):
        part = value.astype(BF16).astype(F32)
        out.append(part)
        value = value - part
    return out


def row_of(shape):
    return lax.broadcasted_iota(jnp.int32, shape, 0)


def stack_rows(rows, shape):
    index = row_of(shape)
    out = jnp.zeros(shape, F32)
    for k, row in rows.items():
        out = jnp.where(index == k, row, out)
    return out


def norms(feats):
    whole = feats + jnp.roll(feats, -3, axis=0)
    squares = jnp.where(row_of(feats.shape) < 3, whole * whole, 0.0)
    return split(jnp.sum(squares, axis=0, keepdims=True), 3)


def row_features(feats):
    shape = feats.shape
    n1, n2, n3 = norms(feats)
    p1, p2, p3 = split(feats[6:7] + feats[7:8] + LOG2_LN2, 3)
    index = row_of(shape)
    double = -2.0 * feats
    with_hi = jnp.where(index < 3, double, jnp.where(index < 6, jnp.roll(double, 3, axis=0), 0.0))
    with_lo = jnp.where(index < 3, jnp.roll(double, -3, axis=0), jnp.where(index < 6, double, 0.0))
    with_norm = stack_rows({0: 1.0, 1: 1.0, 2: 1.0, 3: n1, 4: n2, 5: n3}, shape)
    with_log = stack_rows({0: p1, 1: p2, 2: p3}, shape)
    rows = jnp.swapaxes(jnp.concatenate([with_hi, with_lo, with_norm, with_log], axis=0), 0, 1).astype(BF16)
    index = row_of((DEPTH, LANES))
    pick = jnp.where((index >= 3 * FEATS) & (index < 3 * FEATS + 3), 1.0, 0.0).astype(BF16)
    return rows, jnp.dot(rows, pick, preferred_element_type=F32)


def column_features(feats):
    n1, n2, n3 = norms(feats)
    with_norm = stack_rows({0: n1, 1: n2, 2: n3, 3: 1.0, 4: 1.0, 5: 1.0}, feats.shape)
    columns = jnp.concatenate([feats, feats, with_norm, jnp.zeros(feats.shape, F32)], axis=0).astype(BF16)
    return columns, feats[6:7] + feats[7:8]


def tile_of(rows, row_log, columns, column_log):
    points = columns.shape[1]
    squared = jnp.dot(rows, columns, preferred_element_type=F32)
    scaled = squared * lax.rsqrt(jnp.maximum(squared, SMALLEST))
    logs = jnp.concatenate([row_log] * (points // LANES), axis=1) + column_log
    return ((scaled + LOG2E) * jnp.exp2(logs - scaled)).astype(BF16)


def prepare_kernel(*refs):
    sources, (packed_ref, feats_ref), buffers, sems = refs[:3], refs[3:5], refs[5:8], refs[8]
    copies = [pltpu.make_async_copy(a, b, sems.at[n]) for n, (a, b) in enumerate(zip(sources, buffers))]
    for copy in copies:
        copy.start()
    for copy in copies[:2]:
        copy.wait()
    coords_ref, intensity_ref, start_ref = buffers
    hi, lo = split((coords_ref[...] - 0.5) * SCALE, 2)
    log_hi, log_lo = split(jnp.log2(intensity_ref[...]), 2)
    rows = {k: hi[k : k + 1] for k in range(3)}
    rows.update({3 + k: lo[k : k + 1] for k in range(3)})
    rows.update({6: log_hi, 7: log_lo})
    feats = stack_rows(rows, feats_ref.shape)
    feats_ref[...] = feats.astype(BF16)
    copies[2].wait()
    packed_ref[...] = jnp.concatenate([start_ref[...].astype(F32), feats], axis=0).astype(BF16)


def prepare(coords, intensity, start):
    columns, points = start.shape
    return pl.pallas_call(
        prepare_kernel,
        in_specs=[pl.BlockSpec(memory_space=pltpu.HBM)] * 3,
        out_shape=(pltpu.VMEM((columns + FEATS, points), BF16), pltpu.VMEM((FEATS, points), BF16)),
        scratch_shapes=[
            pltpu.VMEM(coords.shape, F32),
            pltpu.VMEM((1, points), F32),
            pltpu.VMEM(start.shape, BF16),
            pltpu.SemaphoreType.DMA((3,)),
        ],
        name="prepare",
    )(coords, intensity[None], start)


def cost(elements):
    return pl.CostEstimate(flops=40 * elements, bytes_accessed=2 * elements, transcendentals=2 * elements)


def near_kernel(count, feats_ref, *refs):
    packed_refs, (rows_ref, row_logs_ref, columns_ref, logs_ref, cov_ref, part_ref) = refs[:count], refs[count:]
    size, points = part_ref.shape
    rows, row_log = row_features(feats_ref[...].astype(F32))
    rows_ref[...], row_logs_ref[...] = rows, row_log
    made = [column_features(ref[...].astype(F32)[size:]) for ref in packed_refs]
    total = jnp.zeros(part_ref.shape, F32)
    for c, ref in enumerate(packed_refs):
        to = slice(c * points, (c + 1) * points)
        columns_ref[:, to], logs_ref[:, to] = made[c]
        cov_ref[:, to] = tile_of(rows, row_log, *made[c])
        total += lax.dot_general(ref[:size], cov_ref[:, to], NT, preferred_element_type=F32)
    part_ref[...] = total


def near(feats, packed):
    rows, points = packed[0].shape
    total = len(packed) * points
    return pl.pallas_call(
        functools.partial(near_kernel, len(packed)),
        out_shape=(
            pltpu.VMEM((points, DEPTH), BF16),
            pltpu.VMEM((points, LANES), F32),
            pltpu.VMEM((DEPTH, total), BF16),
            pltpu.VMEM((1, total), F32),
            pltpu.VMEM((points, total), BF16),
            pltpu.VMEM((rows - FEATS, points), F32),
        ),
        compiler_params=PARAMS,
        cost_estimate=cost(total * points),
        name="near",
    )(feats, *packed)


def far_kernel(count, near_ref, rows_ref, row_logs_ref, columns_ref, logs_ref, last_ref, *refs):
    feats_refs, packed_refs, (edge_ref, cov_ref, sum_ref, sent_ref) = refs[:count], refs[count:-4], refs[-4:]
    size, points = near_ref.shape
    made = [row_features(ref[...].astype(F32)) for ref in feats_refs]
    columns, logs = [], []
    for c in range(len(packed_refs)):
        to = slice(c * points, (c + 1) * points)
        columns.append(columns_ref[:, to])
        logs.append(logs_ref[:, to])
    last, last_log = column_features(last_ref[...].astype(F32)[size:])
    columns.append(last)
    logs.append(last_log)
    sources = list(packed_refs) + [last_ref]
    vectors = jnp.concatenate([ref[:size] for ref in sources], axis=1)
    edge_ref[...] = tile_of(rows_ref[...], row_logs_ref[...], last, last_log)
    total = near_ref[...] + lax.dot_general(last_ref[:size], edge_ref[...], NT, preferred_element_type=F32)
    sum_ref[0] = total
    sent_ref[0] = total.astype(BF16)
    for k in range(count):
        at = slice(k * points, (k + 1) * points)
        for c in range(len(sources)):
            to = slice(c * points, (c + 1) * points)
            cov_ref[at, to] = tile_of(*made[k], columns[c], logs[c])
        total = lax.dot_general(vectors, cov_ref[at], NT, preferred_element_type=F32)
        sum_ref[k + 1] = total
        sent_ref[k + 1] = total.astype(BF16)


def far(near_part, rows, row_logs, columns, logs, feats, packed, last):
    size, points = near_part.shape
    height, wide = len(feats) * points, (len(packed) + 1) * points
    return pl.pallas_call(
        functools.partial(far_kernel, len(feats)),
        out_shape=(
            pltpu.VMEM((points, points), BF16),
            pltpu.VMEM((height, wide), BF16),
            pltpu.VMEM((1 + len(feats), size, points), F32),
            pltpu.VMEM((1 + len(feats), size, points), BF16),
        ),
        compiler_params=PARAMS,
        cost_estimate=cost((height + points) * wide),
        name="far",
    )(near_part, rows, row_logs, columns, logs, last, *feats, *packed)


def gram_of(product):
    return lax.dot_general(product, product, NT, precision=lax.Precision.HIGHEST, preferred_element_type=F32)


def fold(second_gram, first_gram):
    half = second_gram.shape[0] // 2
    both = jnp.concatenate([second_gram, first_gram], axis=1)
    return jnp.concatenate([both[:half], both[half:]], axis=1)


def unfold(folded):
    size = 2 * folded.shape[0]
    both = jnp.concatenate([folded[:, : 2 * size], folded[:, 2 * size :]], axis=0)
    return both[:, :size], both[:, size:]


def second_kernel(own_ref, *refs):
    part_refs, near_ref, edge_ref, far_ref, outs = refs[:3], refs[3], refs[4], refs[5], refs[6:-2]
    vectors_ref, first_ref = refs[-2:]
    count, size, points = own_ref.shape
    last = len(outs)
    totals = [jnp.zeros((2 * size, points), F32) for _ in outs]
    for k in range(count):
        a, b, c = (ref[k ^ (n + 1)].astype(F32) for n, ref in enumerate(part_refs))
        product = (own_ref[k] + a) + (b + c)
        if k == 0:
            first_ref[...] = product
        vectors = jnp.concatenate(split(product, 2), axis=0).astype(BF16)
        vectors_ref[k] = vectors
        for n in range(1, last + 1):
            to = slice(n * points, (n + 1) * points)
            if k == 0:
                cov = near_ref[:, to] if n < last else edge_ref[...]
            else:
                cov = far_ref[(k - 1) * points : k * points, to]
            totals[n - 1] += jnp.dot(vectors, cov, preferred_element_type=F32)
    for ref, total in zip(outs, totals):
        ref[...] = total[:size] + total[size:]


def second(own, parts, near_cov, edge_cov, far_cov):
    count, size, points = own.shape
    others = far_cov.shape[1] // points - 1
    return pl.pallas_call(
        second_kernel,
        out_shape=[pltpu.VMEM((size, points), F32)] * others
        + [pltpu.VMEM((count, 2 * size, points), BF16), pltpu.VMEM((size, points), F32)],
        compiler_params=PARAMS,
        cost_estimate=cost(count * points * others * points // 8),
        name="second",
    )(own, *parts, near_cov, edge_cov, far_cov)


def kept_kernel(vectors_ref, first_ref, near_ref, far_ref, out_ref, gram_ref):
    count, double, points = vectors_ref.shape
    total = jnp.dot(vectors_ref[0], near_ref[:, :points], preferred_element_type=F32)
    for k in range(1, count):
        cov = far_ref[(k - 1) * points : k * points, :points]
        total += jnp.dot(vectors_ref[k], cov, preferred_element_type=F32)
    out_ref[...] = total[: double // 2] + total[double // 2 :]
    gram_ref[...] = gram_of(first_ref[...])


def kept(vectors, first, near_cov, far_cov):
    size, points = first.shape
    return pl.pallas_call(
        kept_kernel,
        out_shape=(pltpu.VMEM((size, points), F32), pltpu.VMEM((size, size), F32)),
        compiler_params=PARAMS,
        cost_estimate=cost(vectors.shape[0] * points * points // 8),
        name="kept",
    )(vectors, first, near_cov, far_cov)


def gather_kernel(first_ref, own_ref, *refs):
    part_refs, (product_ref, gram_ref) = refs[:-2], refs[-2:]
    product = own_ref[...]
    for ref in part_refs:
        product += ref[...]
    product_ref[...] = product
    gram_ref[...] = fold(gram_of(product), first_ref[...])


def gather_parts(first_gram, own, parts):
    size, points = own.shape
    return pl.pallas_call(
        gather_kernel,
        out_shape=(pltpu.VMEM((size, points), F32), pltpu.VMEM((size // 2, 4 * size), F32)),
        compiler_params=SMALL,
        name="gather_parts",
    )(first_gram, own, *parts)


def row_kernel(packed_ref, feats_ref, out_ref):
    size = out_ref.shape[0]
    rows, row_log = row_features(feats_ref[...].astype(F32))
    out_ref[...] = jnp.zeros(out_ref.shape, F32)

    def step(k, carry):
        packed = packed_ref[k]
        columns, column_log = column_features(packed[size:].astype(F32))
        tile = tile_of(rows, row_log, columns, column_log)
        out_ref[...] += lax.dot_general(packed[:size], tile, NT, preferred_element_type=F32)
        return carry

    lax.fori_loop(0, packed_ref.shape[0], step, 0)


def row_product(packed, feats):
    _, rows, points = packed.shape
    return pl.pallas_call(
        row_kernel,
        out_shape=jax.ShapeDtypeStruct((rows - FEATS, points), F32),
        compiler_params=PARAMS,
        name="row_product",
    )(packed, feats)


def grams_kernel(second_ref, first_ref, gram_ref):
    gram_ref[...] = fold(gram_of(second_ref[...]), gram_of(first_ref[...]))


def grams(second_product, first_product):
    size = first_product.shape[0]
    return pl.pallas_call(
        grams_kernel,
        out_shape=jax.ShapeDtypeStruct((size // 2, 4 * size), F32),
        compiler_params=SMALL,
        name="grams",
    )(second_product, first_product)


def eliminate(gram):
    size = gram.shape[0]
    wide = (size, LANES)
    index = row_of(wide)
    cols = [jnp.broadcast_to(gram[:, k : k + 1], wide) for k in range(size)]
    multipliers, factor_cols = [], []
    scale = jnp.zeros(wide, F32)
    for k in range(size):
        pivot = jnp.broadcast_to(cols[k][k : k + 1], wide)
        root = 1.0 / jnp.sqrt(pivot)
        multiplier = jnp.where(index > k, cols[k] / pivot, 0.0)
        for j in range(k + 1, size):
            cols[j] = cols[j] - multiplier * jnp.broadcast_to(cols[j][k : k + 1], wide)
        multipliers.append(multiplier)
        factor_cols.append(jnp.where(index >= k, cols[k] * root, 0.0))
        scale = jnp.where(index == k, root, scale)
    return multipliers, factor_cols, scale


def finish_kernel(total_points, product_ref, *refs):
    gram_refs, (basis_ref, factor_ref) = refs[:-2], refs[-2:]
    size, points = product_ref.shape
    gram = gram_refs[0][...] + gram_refs[1][...]
    if len(gram_refs) > 2:
        gram = gram + (gram_refs[2][...] + gram_refs[3][...])
    gram, first_gram = unfold(gram / total_points)
    steps, cols, scale = eliminate(gram)
    first_steps, _, first_scale = eliminate(first_gram)
    for at in range(0, points, LANES):
        part = product_ref[:, at : at + LANES]
        for k in range(size):
            part = part - steps[k] * part[k : k + 1]
        basis_ref[:, at : at + LANES] = part * scale
    lane = lax.broadcasted_iota(jnp.int32, (size, LANES), 1)
    factor = jnp.zeros((size, LANES), F32)
    for k in range(size):
        factor = jnp.where(lane == k, cols[k], factor)
    for k in range(size):
        factor = factor - first_steps[k] * factor[k : k + 1]
    factor_ref[...] = (factor * first_scale)[:, :size]


def finish(product, gram_parts, total_points):
    size, points = product.shape
    return pl.pallas_call(
        functools.partial(finish_kernel, total_points),
        out_shape=(jax.ShapeDtypeStruct((size, points), F32), jax.ShapeDtypeStruct((size, size), F32)),
        compiler_params=SMALL,
        name="finish",
    )(product, *gram_parts)


def rounds_of(width):
    bits = [1 << k for k in range(width.bit_length() - 1)][::-1]
    out = []
    while bits:
        take = 1 if len(bits) % 2 else 2
        group, bits = bits[:take], bits[take:]
        out.append([group[0]] if take == 1 else [group[1], group[0], group[0] + group[1]])
    return out


def exchange(value, distance, width):
    return lax.ppermute(value, "wide", [(k, k ^ distance) for k in range(width)])


def sum_parts(value, width):
    rounds = rounds_of(width)[::-1]
    rounds = rounds[:1] + [[d + 1 if d.bit_count() == 1 else d ^ 1 for d in r] for r in rounds[1:]]
    for n, distances in enumerate(rounds):
        parts = [value] + [exchange(value, d, width) for d in distances]
        if n == len(rounds) - 1:
            return parts
        value = parts[1] + parts[0]
        if len(parts) > 2:
            value = value + (parts[3] + parts[2])


def gather_blocks(value, width):
    held = value[None]
    for distances in rounds_of(width):
        held = jnp.concatenate([held] + [exchange(held, d, width) for d in distances], axis=0)
    return held


def body(coords, intensity, start):
    width = lax.axis_size("wide")
    size, points = start.shape
    packed, feats = prepare(coords, intensity, start)
    if width == 16:
        near_steps, far_steps = (1, 2, 3), (13, 4, 9)
        blocks = [packed] + [exchange(packed, d, width) for d in far_steps]
        others = [exchange(feats, d, width) for d in near_steps]
        *features, near_cov, part = near(feats, blocks[:-1])
        edge_cov, far_cov, own, sent = far(part, *features, others, blocks[:-1], blocks[-1])
        parts = [exchange(own if d == 1 else sent, d, width) for d in near_steps]
        *products, vectors, first = second(own, parts, near_cov, edge_cov, far_cov)
        got = [exchange(p, d, width) for p, d in zip(products, far_steps)]
        product, first_gram = kept(vectors, first, near_cov, far_cov)
        product, gram = gather_parts(first_gram, product, got)
    else:
        everything = gather_blocks(packed, width)
        first_product = row_product(everything, feats)
        vectors = gather_blocks(first_product.astype(BF16), width)
        product = row_product(jnp.concatenate([vectors, everything[:, size:]], axis=1), feats)
        gram = grams(product, first_product)
    return finish(product, sum_parts(gram, width), float(points * width))


def solution(mesh):
    placed = (P(None, ("camp", "wide")), P(("camp", "wide")), P(None, ("camp", "wide")))
    return jax.shard_map(
        body,
        mesh=mesh,
        in_specs=placed,
        out_specs=(P(None, ("camp", "wide")), P("camp", None)),
        check_vma=False,
    )
```
